32 devices in a mesh: wide: 8 (over y, x, core), narrow: 4 (over z).
Axes of the slice: x: 2, y: 2, z: 4, core: 2. Of those that a mesh axis runs over, the one named last changes fastest.
Arguments:
- hidden_in: bfloat16 [131072, 768], P(('wide', 'narrow')), may hold values from -6 to 6
- lengths: int32 [256], P(('wide', 'narrow')), may hold values from 16 to 512, as said below
- labels: int32 [256], P(('wide', 'narrow')), may hold values from 0 to 2
- qkv_weight: bfloat16 [768, 2304], replicated, may hold values from -0.21875 to 0.21875
- qkv_bias: float32 [2304], replicated, may hold values from -4 to 4
- out_weight: bfloat16 [768, 768], replicated, may hold values from -0.875 to 0.875
- out_bias: float32 [768], replicated, may hold values from -4 to 4
- attention_gain: float32 [768], replicated, may hold values from 0.5 to 1.5
- attention_shift: float32 [768], replicated, may hold values from -4 to 4
- up_weight: bfloat16 [768, 3072], replicated, may hold values from -0.21875 to 0.21875
- up_bias: float32 [3072], replicated, may hold values from -4 to 4
- down_weight: bfloat16 [3072, 768], replicated, may hold values from -0.109375 to 0.109375
- down_bias: float32 [768], replicated, may hold values from -4 to 4
- output_gain: float32 [768], replicated, may hold values from 0.5 to 1.5
- output_shift: float32 [768], replicated, may hold values from -4 to 4
- pooler_weight: bfloat16 [768, 768], replicated, may hold values from -0.21875 to 0.21875
- pooler_bias: float32 [768], replicated, may hold values from -6 to 6
- ramp_weight: float32 [768, 3], replicated, may hold values from -1.5 to 1.5
- ramp_bias: float32 [3], replicated, may hold values from -6 to 6
Outputs:
- hidden_out: bfloat16 [131072, 768], P(('wide', 'narrow'))
- logits: float32 [256, 3], P(('wide', 'narrow'))
- grad_pooler_weight: float32 [768, 768], replicated
- grad_pooler_bias: float32 [768], replicated
- grad_ramp_weight: float32 [768, 3], replicated
- grad_ramp_bias: float32 [3], replicated
- entropy: float32 [], replicated
The draws below stay inside these ranges and needn't reach their ends.
Inputs may be any that keep to these rules, and one draw needn't show every extreme that they name: `lengths`: every sequence has at least 16 tokens; in every draw some sequence fills its slot of 512.
All inputs are finite; a program needn't handle non-finite values.
Results may differ from the reference program's by a relative error of at most 0.0075.
Values sent between devices are 32-bit elements; how exact they have to be, the bound alone decides.
No kernel may reach another device: no remote copies, remote signals or barrier semaphores. Data moves between devices by JAX's collectives and lax.ppermute only.
A program may use at most 128 MiB of HBM per device.

```python
import jax
import jax.numpy as jnp
from jax import lax

D = 768
HEADS = 12
HEAD_DIM = 64
FF = 3072
CLASSES = 3
SEQ_LEN = 512
SEQ_DEV = 8
N_SEQ = 256
TOKENS = 131072


def draw_lengths(key, part):
    key = jax.random.fold_in(key, 7)
    first_key, second_key = jax.random.split(key)
    shortest = SEQ_LEN // 32
    slots = jnp.arange(N_SEQ)
    device_place = slots // SEQ_DEV
    devices = N_SEQ // SEQ_DEV
    ceiling = shortest + (SEQ_LEN - shortest) * (1 + 2 * device_place) // (2 * devices)
    length_draw = jax.random.randint(first_key, (N_SEQ,), shortest, ceiling + 1)
    chosen = jax.random.randint(second_key, (), 0, N_SEQ)
    return jnp.where(slots == chosen, SEQ_LEN, length_draw).astype(jnp.int32)


def with_ends(drawn, key, low, largest):
    longest = drawn.shape.index(max(drawn.shape))
    spots = []
    for shift in (0, 1):
        where = [jax.random.randint(jax.random.fold_in(key, axis), (), 0, length) for axis, length in enumerate(drawn.shape)]
        where[longest] = (where[longest] + shift) % drawn.shape[longest]
        spots.append(tuple(where))
    return drawn.at[spots[0]].set(low).at[spots[1]].set(largest)


def level_of(own_key, dims, cuts, least, top_value):
    level = 1.0
    for position, shards_of in cuts:
        heights = jax.random.uniform(jax.random.fold_in(jax.random.fold_in(own_key, 6), position), (shards_of,), jnp.float32, least / len(cuts), top_value / len(cuts))
        level = level * jnp.repeat(jnp.exp(heights), dims[position] // shards_of).reshape((-1,) + (1,) * (len(dims) - 1 - position))
    return level


def scatter_about(key, shape, width, reach, shards=(), held_as=jnp.bfloat16):
    drawn = width * jax.random.normal(key, shape, jnp.float32)
    if shards:
        drawn = drawn * level_of(key, shape, shards, -0.22, 0.18)
    return jnp.clip(drawn, -reach, reach).astype(held_as)


def setup_inputs(seed: int = 0) -> dict:
    streams_of = jax.random.split(jax.random.key(seed), 20)
    hidden_in = scatter_about(streams_of[0], (TOKENS, D), 1.0, 6.0, ((0, 32),))
    lengths = draw_lengths(jax.random.fold_in(streams_of[19], 71), 0)
    labels = with_ends(jax.random.randint(streams_of[2], (N_SEQ,), 0, CLASSES), jax.random.fold_in(streams_of[2], 1), 0, CLASSES - 1).astype(jnp.int32)
    qkv_weight = scatter_about(streams_of[3], (D, 3 * D), D ** -0.5, 0.21875)
    qkv_bias = scatter_about(streams_of[4], (3 * D,), 0.3, 4.0, (), jnp.float32)
    out_weight = scatter_about(streams_of[5], (D, D), (D // 16) ** -0.5, 0.875)
    out_bias = scatter_about(streams_of[6], (D,), 0.3, 4.0, (), jnp.float32)
    attention_gain = jnp.clip(1.0 + 0.1 * jax.random.normal(streams_of[7], (D,), jnp.float32), 0.5, 1.5)
    attention_shift = scatter_about(streams_of[8], (D,), 0.3, 4.0, (), jnp.float32)
    up_weight = scatter_about(streams_of[9], (D, FF), D ** -0.5, 0.21875)
    up_bias = scatter_about(streams_of[10], (FF,), 0.3, 4.0, (), jnp.float32)
    down_weight = scatter_about(streams_of[11], (FF, D), FF ** -0.5, 0.109375)
    down_bias = scatter_about(streams_of[12], (D,), 0.3, 4.0, (), jnp.float32)
    output_gain = jnp.clip(1.0 + 0.1 * jax.random.normal(streams_of[13], (D,), jnp.float32), 0.5, 1.5)
    output_shift = scatter_about(streams_of[14], (D,), 0.3, 4.0, (), jnp.float32)
    pooler_weight = scatter_about(streams_of[15], (D, D), D ** -0.5, 0.21875)
    pooler_bias = scatter_about(streams_of[16], (D,), 0.5, 6.0, (), jnp.float32)
    ramp_weight = scatter_about(streams_of[17], (D, CLASSES), 0.1, 1.5, (), jnp.float32)
    ramp_bias = scatter_about(streams_of[18], (CLASSES,), 0.5, 6.0, (), jnp.float32)
    return dict(hidden_in=hidden_in, lengths=lengths, labels=labels, qkv_weight=qkv_weight, qkv_bias=qkv_bias, out_weight=out_weight, out_bias=out_bias, attention_gain=attention_gain, attention_shift=attention_shift, up_weight=up_weight, up_bias=up_bias, down_weight=down_weight, down_bias=down_bias, output_gain=output_gain, output_shift=output_shift, pooler_weight=pooler_weight, pooler_bias=pooler_bias, ramp_weight=ramp_weight, ramp_bias=ramp_bias)


@jax.custom_vjp
def low(v):
    return lax.optimization_barrier(v.astype(jnp.bfloat16)).astype(jnp.float32)

@jax.custom_vjp
def low_back(v):
    return v

def low_keep(v):
    return (low(v), None)

def low_pass(kept, grad):
    return (grad,)

def back_keep(v):
    return (v, None)

def back_low(kept, grad):
    return (low(grad),)
low.defvjp(low_keep, low_pass)
low_back.defvjp(back_keep, back_low)
HIGHEST = lax.Precision.HIGHEST

def matmul(left, right):
    return jnp.dot(left, right, precision=HIGHEST, preferred_element_type=jnp.float32)

def layer_norm(values, gain, shift):
    center = values - lax.optimization_barrier(jnp.mean(values, axis=-1, keepdims=True))
    spread = lax.optimization_barrier(jnp.mean(center * center, axis=-1, keepdims=True))
    return center * lax.rsqrt(spread + 1e-12) * gain + shift

def encode(tokens, length, weights):
    qkv_weight, qkv_bias, out_weight, out_bias, attention_gain, attention_shift, up_weight, up_bias, down_weight, down_bias, output_gain, output_shift = weights
    rows = tokens.shape[0]
    projected = matmul(low(tokens), qkv_weight) + qkv_bias
    queries = low(projected[:, :D]).reshape(rows, HEADS, HEAD_DIM)
    key_rows = low(projected[:, D:2 * D]).reshape(rows, HEADS, HEAD_DIM)
    value_rows = low(projected[:, 2 * D:]).reshape(rows, HEADS, HEAD_DIM)
    scores = jnp.einsum('qhd,khd->hqk', queries, key_rows, precision=HIGHEST) * HEAD_DIM ** (-0.5)
    positions = jnp.arange(rows)
    visible = positions[None, None, :] < length
    scores = jnp.where(visible, scores, jnp.float32(-1000000000.0))
    row_max = lax.optimization_barrier(jnp.max(scores, axis=-1, keepdims=True))
    weights_exp = jnp.exp(scores - row_max)
    attention = low(weights_exp / lax.optimization_barrier(jnp.sum(weights_exp, axis=-1, keepdims=True)))
    context = jnp.einsum('hqk,khd->qhd', attention, value_rows, precision=HIGHEST).reshape(rows, D)
    context = low(context)
    after_attention = layer_norm(tokens + matmul(context, out_weight) + out_bias, attention_gain, attention_shift)
    active = low(jax.nn.gelu(matmul(low(after_attention), up_weight) + up_bias, approximate=False))
    second = matmul(active, down_weight) + down_bias
    return low(layer_norm(after_attention + second, output_gain, output_shift))

def reference(hidden_in, lengths, labels, qkv_weight, qkv_bias, out_weight, out_bias, attention_gain, attention_shift, up_weight, up_bias, down_weight, down_bias, output_gain, output_shift, pooler_weight, pooler_bias, ramp_weight, ramp_bias):
    weights = tuple((matrix.astype(jnp.float32) for matrix in (qkv_weight, qkv_bias, out_weight, out_bias, attention_gain, attention_shift, up_weight, up_bias, down_weight, down_bias, output_gain, output_shift)))
    sequences = hidden_in.astype(jnp.float32).reshape(N_SEQ, SEQ_LEN, D)
    onehot = (labels[:, None] == jnp.arange(CLASSES)[None, :]).astype(jnp.float32)
    ramp_params = (pooler_weight.astype(jnp.float32), pooler_bias, ramp_weight, ramp_bias)

    def forward(params):
        encoded = lax.map(lambda carried: encode(carried[0], carried[1], weights), (sequences, lengths))
        leading = encoded[:, 0, :]
        before_tanh = low_back(matmul(leading, params[0]) + params[1])
        pooled = jnp.tanh(before_tanh)
        scored = matmul(pooled, params[2]) + params[3]
        total = jnp.sum(jax.nn.logsumexp(scored, axis=1) - lax.optimization_barrier(jnp.sum(onehot * scored, axis=1)))
        return (total, (encoded, scored))
    loss_total, pullback, extras = jax.vjp(forward, ramp_params, has_aux=True)
    encoded, logits = extras
    gradients = pullback(jnp.float32(1.0))[0]
    hidden_out = encoded.astype(jnp.bfloat16).reshape(TOKENS, D)
    log_probs = jax.nn.log_softmax(logits, axis=1)
    row_entropy = -lax.optimization_barrier(jnp.sum(jnp.exp(log_probs) * log_probs, axis=1))
    length_float = lengths.astype(jnp.float32)
    entropy = jnp.sum(length_float * row_entropy) / jnp.sum(length_float)
    return (hidden_out, logits, gradients[0], gradients[1], gradients[2], gradients[3], entropy)
```

```python
import functools

import jax
import jax.numpy as jnp
from jax import lax
from jax.experimental import pallas as pl
from jax.experimental.pallas import tpu as pltpu
from jax.sharding import PartitionSpec as P

D = 768
HEADS = 12
HEAD_DIM = 64
FF = 3072
CLASSES = 3
LANES = 128
PAIRS = HEADS // 2
KEY_BLOCK = 128
CHUNK = 512
EXTRA = 128

AXES = ("wide", "narrow")
HIGHEST = lax.Precision.HIGHEST
ROWS_BY_ROWS = (((1,), (1,)), ((), ()))
COLS_BY_COLS = (((0,), (0,)), ((), ()))
f32 = jnp.float32
bf16 = jnp.bfloat16


def layer_norm(values, gain, shift):
    center = values - jnp.mean(values, axis=-1, keepdims=True)
    spread = jnp.mean(center * center, axis=-1, keepdims=True)
    return center * lax.rsqrt(spread + 1e-12) * gain + shift


def gelu(values):
    half = 0.5 * values
    return half + half * lax.erf(values * 0.7071067811865476)


def project_keys(x_ref, slot, blocks, length, weight, bias, keys, values):
    rows = blocks * KEY_BLOCK
    tokens = x_ref[slot, :rows, :]
    visible = lax.broadcasted_iota(jnp.int32, (rows, 1), 0) < length
    key_rows = jnp.dot(tokens, weight[:, D : 2 * D], preferred_element_type=f32) + bias[:, D : 2 * D]
    keys[slot, :rows, :] = jnp.where(visible, key_rows, key_rows[0:1, :]).astype(bf16)
    value_rows = jnp.dot(tokens, weight[:, 2 * D :], preferred_element_type=f32) + bias[:, 2 * D :]
    values[slot, :rows, :] = jnp.where(visible, value_rows, 0.0).astype(bf16)


def attend(queries, keys, values, slot, blocks, length, context, row, rows):
    low = lax.broadcasted_iota(jnp.int32, (1, LANES), 1) < HEAD_DIM
    zero = jnp.zeros((), bf16)

    def apart(block):
        return jnp.concatenate([jnp.where(low, block, zero), jnp.where(low, zero, block)], axis=0)

    ones = apart(jnp.ones((KEY_BLOCK, LANES), bf16))
    last = (blocks - 1) * KEY_BLOCK + lax.broadcasted_iota(jnp.int32, (KEY_BLOCK, LANES), 0) < length
    ones_last = apart(jnp.where(last, 1.0, 0.0).astype(bf16))
    for pair in range(PAIRS):
        lanes = slice(pair * LANES, (pair + 1) * LANES)
        mine = queries[row : row + rows, lanes]
        scores = []
        for block in range(blocks):
            spot = slice(block * KEY_BLOCK, (block + 1) * KEY_BLOCK)
            scores.append(
                lax.dot_general(mine, apart(keys[slot, spot, lanes]), ROWS_BY_ROWS, preferred_element_type=f32)
            )
        top = functools.reduce(jnp.maximum, scores)
        top_low = jnp.max(top[:, :KEY_BLOCK], axis=-1, keepdims=True)
        top_high = jnp.max(top[:, KEY_BLOCK:], axis=-1, keepdims=True)
        total = None
        for block in range(blocks):
            spot = slice(block * KEY_BLOCK, (block + 1) * KEY_BLOCK)
            weights = jnp.concatenate(
                [
                    jnp.exp(scores[block][:, :KEY_BLOCK] - top_low).astype(bf16),
                    jnp.exp(scores[block][:, KEY_BLOCK:] - top_high).astype(bf16),
                ],
                axis=1,
            )
            held = jnp.concatenate(
                [apart(values[slot, spot, lanes]), ones_last if block == blocks - 1 else ones], axis=1
            )
            term = jnp.dot(weights, held, preferred_element_type=f32)
            total = term if total is None else total + term
        context[row : row + rows, lanes] = (total[:, :LANES] / total[:, LANES:]).astype(bf16)


def finish(tokens, context, out_w, up_w, down_w, biases, active):
    out_bias, attention_gain, attention_shift, up_bias, down_bias, output_gain, output_shift = biases
    attended = jnp.dot(context[...], out_w[...], preferred_element_type=f32) + out_bias[...]
    after = layer_norm(tokens.astype(f32) + attended, attention_gain[...], attention_shift[...])
    after_low = after.astype(bf16)
    for start in range(0, FF, CHUNK):
        spot = slice(start, start + CHUNK)
        expanded = jnp.dot(after_low, up_w[:, spot], preferred_element_type=f32) + up_bias[:, spot]
        active[:, spot] = gelu(expanded).astype(bf16)
    second = jnp.dot(active[...], down_w[...], preferred_element_type=f32) + down_bias[...]
    return layer_norm(after + second, output_gain[...], output_shift[...]).astype(bf16)


def first_kernel(
    half,
    lengths, labels,
    x_hbm, qkv_hbm, out_hbm, up_hbm, down_hbm,
    qkv_bias, *rest,
):
    biases = rest[:7]
    hidden_hbm, keys_hbm, values_hbm, lead = rest[7:11]
    x, qkv_w, out_w, up_w, down_w, keys, values, queries, context, active, result, load_sem, x_sem, store_sem, kv_sem = rest[11:]
    slots = x.shape[0]
    tiles = slots // 2

    def load_x(slot):
        return pltpu.make_async_copy(x_hbm.at[slot], x.at[slot], x_sem.at[slot])

    weights = [(qkv_hbm, qkv_w), (out_hbm, out_w), (up_hbm, up_w), (down_hbm, down_w)]
    loads = [pltpu.make_async_copy(a, b, load_sem.at[i]) for i, (a, b) in enumerate(weights)]

    def store(tile):
        return pltpu.make_async_copy(
            result.at[tile], hidden_hbm.at[pl.ds(2 * tile, 2), pl.ds(0, half), :], store_sem.at[tile]
        )

    def store_kv(slot):
        return (
            pltpu.make_async_copy(keys.at[slot], keys_hbm.at[slot], kv_sem.at[0, slot]),
            pltpu.make_async_copy(values.at[slot], values_hbm.at[slot], kv_sem.at[1, slot]),
        )

    for slot in range(2):
        load_x(slot).start()
    loads[0].start()
    for slot in range(2, slots):
        load_x(slot).start()
    for load in loads[1:]:
        load.start()
    loads[0].wait()

    def tile_step(tile, carry):
        for j in range(2):
            load_x(2 * tile + j).wait()
        tokens = x[pl.ds(2 * tile, 2), :half, :].reshape(2 * half, D)
        projected = jnp.dot(tokens, qkv_w[:, :D], preferred_element_type=f32) + qkv_bias[:, :D]
        queries[...] = projected.astype(bf16) * jnp.asarray(HEAD_DIM ** (-0.5), bf16)
        for j in range(2):
            slot = 2 * tile + j
            length = lengths[slot]
            count = (length + KEY_BLOCK - 1) // KEY_BLOCK
            for blocks in range(1, x.shape[1] // KEY_BLOCK + 1):

                @pl.when(count == blocks)
                def _():
                    project_keys(x, slot, blocks, length, qkv_w, qkv_bias, keys, values)
                    attend(queries, keys, values, slot, blocks, length, context, j * half, half)

            for copy in store_kv(slot):
                copy.start()

        @pl.when(tile == 0)
        def _():
            for load in loads[1:]:
                load.wait()

        done = finish(tokens, context, out_w, up_w, down_w, biases, active)
        result[tile] = done.reshape(2, half, D)
        for j in range(2):
            slot = 2 * tile + j
            place = lax.broadcasted_iota(jnp.int32, (1, EXTRA), 1)
            facts = jnp.where(place == 0, lengths[slot], labels[slot]).astype(f32)
            lead[pl.ds(slot, 1), :] = jnp.concatenate([done[j * half : j * half + 1, :].astype(f32), facts], axis=1)
        store(tile).start()
        return carry

    lax.fori_loop(0, tiles, tile_step, 0)
    for tile in range(tiles):
        store(tile).wait()
    for slot in range(slots):
        for copy in store_kv(slot):
            copy.wait()


def second_kernel(
    half,
    lengths,
    x_hbm, keys_hbm, values_hbm, qkv_hbm, out_hbm, up_hbm, down_hbm, hidden_in_place,
    qkv_bias, *rest,
):
    biases = rest[:7]
    (hidden_hbm,) = rest[7:8]
    x, q_w, out_w, up_w, down_w, keys, values, queries, context, active, result, load_sem, x_sem, store_sem, kv_sem = rest[8:]
    slots = x.shape[0]
    tiles = slots // 2

    def load_x(slot):
        return pltpu.make_async_copy(x_hbm.at[slot, pl.ds(half, half), :], x.at[slot], x_sem.at[slot])

    def load_kv(slot):
        return (
            pltpu.make_async_copy(keys_hbm.at[slot], keys.at[slot], kv_sem.at[0, slot]),
            pltpu.make_async_copy(values_hbm.at[slot], values.at[slot], kv_sem.at[1, slot]),
        )

    weights = [(qkv_hbm.at[:, pl.ds(0, D)], q_w), (out_hbm, out_w), (up_hbm, up_w), (down_hbm, down_w)]
    loads = [pltpu.make_async_copy(a, b, load_sem.at[i]) for i, (a, b) in enumerate(weights)]

    def store(tile):
        return pltpu.make_async_copy(
            result.at[tile], hidden_hbm.at[pl.ds(2 * tile, 2), pl.ds(half, half), :], store_sem.at[tile]
        )

    def load_slot(slot):
        load_x(slot).start()
        for copy in load_kv(slot):
            copy.start()

    for slot in range(2):
        load_x(slot).start()
    loads[0].start()
    for slot in range(2):
        for copy in load_kv(slot):
            copy.start()
    for load in loads[1:]:
        load.start()
    for slot in range(2, slots):
        load_slot(slot)
    loads[0].wait()

    def tile_step(tile, carry):
        for j in range(2):
            load_x(2 * tile + j).wait()
        tokens = x[pl.ds(2 * tile, 2), :, :].reshape(2 * half, D)
        projected = jnp.dot(tokens, q_w[...], preferred_element_type=f32) + qkv_bias[:, :D]
        queries[...] = projected.astype(bf16) * jnp.asarray(HEAD_DIM ** (-0.5), bf16)
        for j in range(2):
            slot = 2 * tile + j
            for copy in load_kv(slot):
                copy.wait()
            length = lengths[slot]
            count = (length + KEY_BLOCK - 1) // KEY_BLOCK
            for blocks in range(1, keys.shape[1] // KEY_BLOCK + 1):

                @pl.when(count == blocks)
                def _():
                    attend(queries, keys, values, slot, blocks, length, context, j * half, half)

        @pl.when(tile == 0)
        def _():
            for load in loads[1:]:
                load.wait()

        done = finish(tokens, context, out_w, up_w, down_w, biases, active)
        result[tile] = done.reshape(2, half, D)
        store(tile).start()
        return carry

    lax.fori_loop(0, tiles, tile_step, 0)
    for tile in range(tiles):
        store(tile).wait()


def ramp_kernel(gathered, pooler_w, pooler_b, ramp_w, ramp_b, logits_out, gpw_out, gpb_out, grw_out, grb_out, entropy_out, scored):
    own = logits_out.shape[0]
    leading = gathered[:, :D].astype(bf16)
    lengths = gathered[:, D : D + 1]
    labels = gathered[:, D + 1 : D + 2]
    pooled = jnp.tanh(jnp.dot(leading, pooler_w[...], preferred_element_type=f32) + pooler_b[...])
    logits = jnp.dot(pooled, ramp_w[...], precision=HIGHEST, preferred_element_type=f32) + ramp_b[...]
    scored[...] = logits
    wide, narrow = lax.axis_index(AXES[0]), lax.axis_index(AXES[1])
    place = wide * lax.axis_size(AXES[1]) + narrow
    logits_out[...] = scored[pl.ds(place * own, own), :]
    shifted = logits - jnp.max(logits, axis=1, keepdims=True)
    powers = jnp.exp(shifted)
    total = jnp.sum(powers, axis=1, keepdims=True)
    probs = powers / total
    classes = lax.broadcasted_iota(jnp.int32, logits.shape, 1).astype(f32)
    dlogits = probs - jnp.where(classes == labels, 1.0, 0.0)
    grw_out[...] = lax.dot_general(pooled, dlogits, COLS_BY_COLS, precision=HIGHEST, preferred_element_type=f32)
    grb_out[...] = jnp.sum(dlogits, axis=0, keepdims=True)
    back = lax.dot_general(dlogits, ramp_w[...], ROWS_BY_ROWS, precision=HIGHEST, preferred_element_type=f32)
    pooled_grad = (back * (1.0 - pooled * pooled)).astype(bf16)
    gpw_out[...] = lax.dot_general(leading, pooled_grad, COLS_BY_COLS, preferred_element_type=f32)
    gpb_out[...] = jnp.sum(pooled_grad.astype(f32), axis=0, keepdims=True)
    log_probs = shifted - jnp.log(total)
    row_entropy = -jnp.sum(jnp.exp(log_probs) * log_probs, axis=1, keepdims=True)
    entropy_out[...] = jnp.sum(lengths * row_entropy, axis=0, keepdims=True) / jnp.sum(lengths, axis=0, keepdims=True)


VMEM_LIMIT = 56 * 1024 * 1024


def local(
    hidden_in, lengths, labels,
    qkv_weight, qkv_bias, out_weight, out_bias, attention_gain, attention_shift,
    up_weight, up_bias, down_weight, down_bias, output_gain, output_shift,
    pooler_weight, pooler_bias, ramp_weight, ramp_bias,
):
    slots = lengths.shape[0]
    length = hidden_in.shape[0] // slots
    half = length // 2
    sequences = hidden_in.reshape(slots, length, D)
    row = lambda vector: vector.reshape(1, -1)
    biases = [row(v) for v in (qkv_bias, out_bias, attention_gain, attention_shift, up_bias, down_bias, output_gain, output_shift)]
    anywhere = pl.BlockSpec(memory_space=pl.ANY)
    scalars = pl.BlockSpec(memory_space=pltpu.SMEM)
    vmem = pl.BlockSpec(memory_space=pltpu.VMEM)
    dma = pltpu.SemaphoreType.DMA
    dense = 2 * slots * half * D * (2 * D + 2 * FF)
    attention = 2 * 2 * slots * half * length * D
    common = [
        pltpu.VMEM((2 * half, D), bf16),
        pltpu.VMEM((2 * half, D), bf16),
        pltpu.VMEM((2 * half, FF), bf16),
        pltpu.VMEM((slots // 2, 2, half, D), bf16),
        dma((4,)),
        dma((slots,)),
        dma((slots // 2,)),
        dma((2, slots)),
    ]
    weight_scratch = [pltpu.VMEM((D, D), bf16), pltpu.VMEM((D, FF), bf16), pltpu.VMEM((FF, D), bf16)]
    kv_shape = (slots, length, D)
    hidden, keys, values, lead = pl.pallas_call(
        functools.partial(first_kernel, half),
        name="first_half",
        out_shape=[
            jax.ShapeDtypeStruct(kv_shape, bf16),
            jax.ShapeDtypeStruct(kv_shape, bf16),
            jax.ShapeDtypeStruct(kv_shape, bf16),
            jax.ShapeDtypeStruct((slots, D + EXTRA), f32),
        ],
        in_specs=[scalars] * 2 + [anywhere] * 5 + [vmem] * 8,
        out_specs=[anywhere] * 3 + [vmem],
        scratch_shapes=[pltpu.VMEM(kv_shape, bf16), pltpu.VMEM((D, 3 * D), bf16)]
        + weight_scratch
        + [pltpu.VMEM(kv_shape, bf16)] * 2
        + common,
        compiler_params=pltpu.CompilerParams(vmem_limit_bytes=VMEM_LIMIT),
        cost_estimate=pl.CostEstimate(flops=dense + attention, bytes_accessed=50_000_000, transcendentals=0),
    )(lengths, labels, sequences, qkv_weight, out_weight, up_weight, down_weight, *biases)
    gathered = lax.all_gather(lead, AXES, axis=0, tiled=True)
    hidden = pl.pallas_call(
        functools.partial(second_kernel, half),
        name="second_half",
        out_shape=jax.ShapeDtypeStruct(kv_shape, bf16),
        in_specs=[scalars] + [anywhere] * 8 + [vmem] * 8,
        out_specs=anywhere,
        scratch_shapes=[pltpu.VMEM((slots, half, D), bf16), pltpu.VMEM((D, D), bf16)]
        + weight_scratch
        + [pltpu.VMEM(kv_shape, bf16)] * 2
        + common,
        input_output_aliases={8: 0},
        compiler_params=pltpu.CompilerParams(vmem_limit_bytes=VMEM_LIMIT),
        cost_estimate=pl.CostEstimate(flops=dense + attention, bytes_accessed=50_000_000, transcendentals=0),
    )(lengths, sequences, keys, values, qkv_weight, out_weight, up_weight, down_weight, hidden, *biases)
    one = lambda *shape: jax.ShapeDtypeStruct(shape, f32)
    logits, gpw, gpb, grw, grb, entropy = pl.pallas_call(
        ramp_kernel,
        name="off_ramp",
        out_shape=[one(slots, CLASSES), one(D, D), one(1, D), one(D, CLASSES), one(1, CLASSES), one(1, 1)],
        in_specs=[vmem] * 5,
        out_specs=[vmem] * 6,
        scratch_shapes=[pltpu.VMEM((gathered.shape[0], CLASSES), f32)],
        compiler_params=pltpu.CompilerParams(vmem_limit_bytes=VMEM_LIMIT),
    )(gathered, pooler_weight, row(pooler_bias), ramp_weight, row(ramp_bias))
    return (
        hidden.reshape(hidden_in.shape),
        logits,
        gpw,
        gpb.reshape(D),
        grw,
        grb.reshape(CLASSES),
        entropy.reshape(()),
    )


def solution(mesh):
    spread = P(AXES)
    placed = (P(AXES, None), spread, spread) + (P(),) * 16
    return jax.shard_map(
        local,
        mesh=mesh,
        in_specs=placed,
        out_specs=(P(AXES, None), P(AXES, None), P(), P(), P(), P(), P()),
        check_vma=False,
    )
```

```python
import functools

import jax
import jax.numpy as jnp
from jax import lax
from jax.experimental import pallas as pl
from jax.experimental.pallas import tpu as pltpu
from jax.sharding import PartitionSpec as P

D = 768
HEADS = 12
HEAD_DIM = 64
FF = 3072
CLASSES = 3
LANES = 128
KEY_BLOCK = 128
QUAD = 2 * LANES
GROUP = 4
EXTRA = 128
TILES = 2

AXES = ("wide", "narrow")
HIGHEST = lax.Precision.HIGHEST
ROWS_BY_ROWS = (((1,), (1,)), ((), ()))
COLS_BY_COLS = (((0,), (0,)), ((), ()))
f32 = jnp.float32
bf16 = jnp.bfloat16


def product(left, right):
    return jnp.dot(left, right, preferred_element_type=f32)


def layer_norm(values, gain, shift):
    center = values - jnp.mean(values, axis=-1, keepdims=True)
    spread = jnp.mean(center * center, axis=-1, keepdims=True)
    return center * lax.rsqrt(spread + 1e-12) * gain + shift


def gelu(values):
    half = 0.5 * values
    return half + half * lax.erf(values * 0.7071067811865476)


def blocks_of(length):
    return (length + KEY_BLOCK - 1) // KEY_BLOCK


def project(tile, x, load_x, lengths, qkv_w, qkv_bias, table, queries, keys, values):
    slots, length = x.shape[0] // TILES, x.shape[1]
    per_slot = length // KEY_BLOCK
    for entry in range(slots * per_slot + GROUP):
        table[entry] = 1
    total = 0
    for slot in range(slots):
        for block in range(per_slot):
            table[total + block] = slot * per_slot + block
        total = total + blocks_of(lengths[slots * tile + slot])

    def keys_step(group, carry):
        tokens = []
        for i in range(GROUP):
            entry = table[group * GROUP + i]
            slot = slots * tile + entry // per_slot
            row = pl.multiple_of(entry % per_slot * KEY_BLOCK, KEY_BLOCK)

            @pl.when(row == 0)
            def _():
                load_x(slot).wait()

        for i in range(GROUP):
            entry = table[group * GROUP + i]
            slot = slots * tile + entry // per_slot
            row = pl.multiple_of(entry % per_slot * KEY_BLOCK, KEY_BLOCK)
            tokens.append(x[slot, pl.ds(row, KEY_BLOCK), :])
        tokens = jnp.concatenate(tokens, axis=0)
        for kept, start in ((keys, D), (values, 2 * D)):
            lanes = slice(start, start + D)
            found = (product(tokens, qkv_w[:, lanes]) + qkv_bias[:, lanes]).astype(bf16)
            for i in range(GROUP):
                row = pl.multiple_of(table[group * GROUP + i] * KEY_BLOCK, KEY_BLOCK)
                kept[pl.ds(row, KEY_BLOCK), :] = found[i * KEY_BLOCK : (i + 1) * KEY_BLOCK]
        return carry

    lax.fori_loop(0, (total + GROUP - 1) // GROUP, keys_step, 0)

    def queries_step(step, carry):
        tokens = x[pl.ds(slots * tile + 2 * step, 2)].reshape(2 * length, D)
        rows = pl.ds(pl.multiple_of(2 * length * step, 2 * length), 2 * length)
        for start in range(0, D, QUAD):
            lanes = slice(start, start + QUAD)
            found = (product(tokens, qkv_w[:, lanes]) + qkv_bias[:, lanes]).astype(bf16)
            queries[rows, lanes] = found * jnp.asarray(HEAD_DIM ** (-0.5), bf16)
        return carry

    lax.fori_loop(0, slots // 2, queries_step, 0)


def attend(slot, blocks, length, queries, keys, values, contexts):
    low = lax.broadcasted_iota(jnp.int32, (1, LANES), 1) < HEAD_DIM
    zero = jnp.zeros((), bf16)
    half = contexts[0].shape[0]
    seen = blocks * KEY_BLOCK
    base = slot * 2 * half

    def apart(block):
        return jnp.concatenate([jnp.where(low, block, zero), jnp.where(low, zero, block)], axis=0)

    visible = seen - KEY_BLOCK + lax.broadcasted_iota(jnp.int32, (KEY_BLOCK, LANES), 0) < length
    ones = apart(jnp.ones((KEY_BLOCK, LANES), bf16))
    ones_last = apart(jnp.where(visible, 1.0, 0.0).astype(bf16))
    for pair in range(0, D, LANES):
        lanes = slice(pair, pair + LANES)
        key_blocks, value_blocks = [], []
        for start in range(0, seen, KEY_BLOCK):
            rows = pl.ds(pl.multiple_of(base + start, KEY_BLOCK), KEY_BLOCK)
            key_block, value_block, counted = keys[rows, lanes], values[rows, lanes], ones
            if start == 0:
                first_key = key_block[0:1, :]
            if start + KEY_BLOCK == seen:
                key_block = jnp.where(visible, key_block, first_key)
                value_block = jnp.where(visible, value_block, zero)
                counted = ones_last
            key_blocks.append(apart(key_block))
            value_blocks.append(jnp.concatenate([apart(value_block), counted], axis=1))
        for part, context in enumerate(contexts):
            rows = pl.ds(pl.multiple_of(base + part * half, half), half)
            mine = queries[rows, lanes]
            scores = [lax.dot_general(mine, block, ROWS_BY_ROWS, preferred_element_type=f32) for block in key_blocks]
            top = functools.reduce(jnp.maximum, scores)
            top_low = jnp.max(top[:, :KEY_BLOCK], axis=-1, keepdims=True)
            top_high = jnp.max(top[:, KEY_BLOCK:], axis=-1, keepdims=True)
            total = None
            for score, block in zip(scores, value_blocks):
                weights = jnp.concatenate(
                    [
                        jnp.exp(score[:, :KEY_BLOCK] - top_low).astype(bf16),
                        jnp.exp(score[:, KEY_BLOCK:] - top_high).astype(bf16),
                    ],
                    axis=1,
                )
                term = product(weights, block)
                total = term if total is None else total + term
            context[:, lanes] = (total[:, :LANES] / total[:, LANES:]).astype(bf16)


def finish_tile(tile, first, x, context, weights, vectors, active, after, result, emit=None):
    out_w, up_w, down_w = weights
    out_bias, attention_gain, attention_shift, up_bias, down_bias, output_gain, output_shift = vectors
    per_tile, half = result.shape[1:3]
    for j in range(per_tile):
        rows = slice(j * half, (j + 1) * half)
        attended = product(context(per_tile * tile + j), out_w[...]) + out_bias
        tokens = x[per_tile * tile + j, first : first + half, :].astype(f32)
        after[rows, :] = layer_norm(tokens + attended, attention_gain, attention_shift)
    total = per_tile * half
    for chunk in range(FF // D):
        spot = slice(chunk * D, (chunk + 1) * D)
        for j in range(0, per_tile, 2):
            rows = slice(j * half, (j + 2) * half)
            expanded = product(after[rows, :].astype(bf16), up_w[:, spot]) + up_bias[:, spot]
            active[chunk * total + j * half : chunk * total + (j + 2) * half, :] = gelu(expanded).astype(bf16)
    for j in range(per_tile):
        rows = slice(j * half, (j + 1) * half)
        spread = [active[chunk * total + j * half : chunk * total + (j + 1) * half, :] for chunk in range(FF // D)]
        second = product(jnp.concatenate(spread, axis=1), down_w[...]) + down_bias
        done = layer_norm(after[rows, :] + second, output_gain, output_shift).astype(bf16)
        result[tile, j] = done
        if emit is not None:
            emit(per_tile * tile + j, done)


def vectors_of(held):
    widths = (3 * D, D, D, D, FF, D, D, D)
    return [held[i : i + 1, :width] for i, width in enumerate(widths)]


def first_kernel(lengths, labels, x_hbm, qkv_hbm, out_hbm, up_hbm, down_hbm, *rest):
    vectors_hbm = rest[:8]
    hidden_hbm, leads, x, later, out_w, up_w, down_w, held = rest[8:16]
    qkv_w, lead, context, table, queries, keys, values, active, after, result, load_sem, x_sem, store_sem, vector_sem = rest[16:]
    slots = x.shape[0]
    per_tile, half = result.shape[1:3]

    def load_x(slot):
        return pltpu.make_async_copy(x_hbm.at[slot], x.at[slot], x_sem.at[slot])

    sources = [(qkv_hbm, qkv_w), (out_hbm, out_w), (up_hbm, up_w), (down_hbm, down_w)]
    loads = [pltpu.make_async_copy(a, b, load_sem.at[i]) for i, (a, b) in enumerate(sources)]
    small = [
        pltpu.make_async_copy(ref, held.at[i, pl.ds(0, ref.shape[0])], vector_sem.at[i])
        for i, ref in enumerate(vectors_hbm)
    ]
    loads[0].start()
    load_x(0).start()
    for copy in small:
        copy.start()
    for slot in range(1, slots):
        load_x(slot).start()
    for load in loads[1:]:
        load.start()

    def store(tile):
        return pltpu.make_async_copy(
            result.at[tile], hidden_hbm.at[pl.ds(per_tile * tile, per_tile), pl.ds(0, half), :], store_sem.at[tile]
        )

    for copy in small:
        copy.wait()
    loads[0].wait()
    vectors = vectors_of(held)

    def attention_step(tile):
        def step(j, carry):
            slot = per_tile * tile + j
            for blocks in range(1, x.shape[1] // KEY_BLOCK + 1):

                @pl.when(blocks_of(lengths[slot]) == blocks)
                def _():
                    attend(j, blocks, lengths[slot], queries, keys, values, (context.at[j], later.at[slot]))

            return carry

        return step

    def emit(slot, done):
        place = lax.broadcasted_iota(jnp.int32, (1, EXTRA), 1)
        facts = jnp.where(place == 0, lengths[slot], labels[slot]).astype(f32)
        lead[pl.ds(slot, 1), :] = jnp.concatenate([done[0:1, :].astype(f32), facts], axis=1)

    def tile_step(tile, carry):
        project(tile, x, load_x, lengths, qkv_w, vectors[0], table, queries, keys, values)
        lax.fori_loop(0, per_tile, attention_step(tile), 0)

        @pl.when(tile == 0)
        def _():
            for load in loads[1:]:
                load.wait()

        mine = lambda slot: context[slot - per_tile * tile]
        finish_tile(tile, 0, x, mine, (out_w, up_w, down_w), vectors[1:], active, after, result, emit)
        store(tile).start()
        return carry

    lax.fori_loop(0, TILES, tile_step, 0)
    for device in range(leads.shape[0]):
        leads[device] = lead[...]
    for tile in range(TILES):
        store(tile).wait()


def second_kernel(x, context, out_w, up_w, down_w, held, hidden_in_place, hidden_hbm, active, after, result, store_sem):
    per_tile, half = result.shape[1:3]
    vectors = vectors_of(held)

    def store(tile):
        return pltpu.make_async_copy(
            result.at[tile], hidden_hbm.at[pl.ds(per_tile * tile, per_tile), pl.ds(half, half), :], store_sem.at[tile]
        )

    def tile_step(tile, carry):
        finish_tile(tile, half, x, lambda slot: context[slot], (out_w, up_w, down_w), vectors[1:], active, after, result)
        store(tile).start()
        return carry

    lax.fori_loop(0, TILES, tile_step, 0)
    for tile in range(TILES):
        store(tile).wait()


def ramp_kernel(gathered, pooler_w, pooler_b, ramp_t, ramp_b, logits_out, gpw_out, gpb_out, grw_out, grb_out, entropy_out, scored):
    own = logits_out.shape[1]
    leading = gathered[:, :D].astype(bf16)
    lengths = gathered[:, D : D + 1]
    labels = gathered[:, D + 1 : D + 2]
    pooled = jnp.tanh(product(leading, pooler_w[...]) + pooler_b[...].reshape(1, -1))
    logits = lax.dot_general(pooled, ramp_t[...], ROWS_BY_ROWS, precision=HIGHEST, preferred_element_type=f32)
    logits = logits + ramp_b[...].reshape(1, -1)
    scored[...] = logits
    wide, narrow = lax.axis_index(AXES[0]), lax.axis_index(AXES[1])
    place = wide * lax.axis_size(AXES[1]) + narrow
    logits_out[...] = scored[pl.ds(pl.multiple_of(place * own, own), own), :].T
    shifted = logits - jnp.max(logits, axis=1, keepdims=True)
    powers = jnp.exp(shifted)
    total = jnp.sum(powers, axis=1, keepdims=True)
    probs = powers / total
    classes = lax.broadcasted_iota(jnp.int32, logits.shape, 1).astype(f32)
    dlogits = probs - jnp.where(classes == labels, 1.0, 0.0)
    grw_out[...] = lax.dot_general(dlogits, pooled, COLS_BY_COLS, precision=HIGHEST, preferred_element_type=f32)
    grb_out[...] = jnp.sum(dlogits, axis=0)
    back = jnp.dot(dlogits, ramp_t[...], precision=HIGHEST, preferred_element_type=f32)
    pooled_grad = (back * (1.0 - pooled * pooled)).astype(bf16)
    gpw_out[...] = lax.dot_general(leading, pooled_grad, COLS_BY_COLS, preferred_element_type=f32)
    gpb_out[...] = jnp.sum(pooled_grad.astype(f32), axis=0)
    log_probs = shifted - jnp.log(total)
    row_entropy = -jnp.sum(jnp.exp(log_probs) * log_probs, axis=1, keepdims=True)
    entropy_out[...] = jnp.sum(lengths * row_entropy, axis=0, keepdims=True) / jnp.sum(lengths, axis=0, keepdims=True)


VMEM_LIMIT = 40 * 1024 * 1024


def local(
    hidden_in, lengths, labels,
    qkv_weight, qkv_bias, out_weight, out_bias, attention_gain, attention_shift,
    up_weight, up_bias, down_weight, down_bias, output_gain, output_shift,
    pooler_weight, pooler_bias, ramp_weight, ramp_bias,
):
    slots = lengths.shape[0]
    length = hidden_in.shape[0] // slots
    half = length // 2
    rows = slots // TILES * half
    shape = (slots, length, D)
    devices = lax.axis_size(AXES)
    sequences = hidden_in.reshape(shape)
    vectors = (qkv_bias, out_bias, attention_gain, attention_shift, up_bias, down_bias, output_gain, output_shift)
    anywhere = pl.BlockSpec(memory_space=pltpu.HBM)
    in_hbm = lambda array: pltpu.with_memory_space_constraint(array, pltpu.HBM)
    scalars = pl.BlockSpec(memory_space=pltpu.SMEM)
    vmem = pl.BlockSpec(memory_space=pltpu.VMEM)
    dma = pltpu.SemaphoreType.DMA
    kept = [
        pltpu.VMEM(shape, bf16),
        pltpu.VMEM((slots, half, D), bf16),
        pltpu.VMEM((D, D), bf16),
        pltpu.VMEM((D, FF), bf16),
        pltpu.VMEM((FF, D), bf16),
        pltpu.VMEM((len(vectors), FF), f32),
    ]
    common = [
        pltpu.VMEM((rows * FF // D, D), bf16),
        pltpu.VMEM((rows, D), f32),
        pltpu.VMEM((TILES, slots // TILES, half, D), bf16),
    ]
    cost = pl.CostEstimate(
        flops=2 * slots * half * D * (2 * D + 2 * FF + 2 * length), bytes_accessed=30_000_000, transcendentals=0
    )
    params = pltpu.CompilerParams(vmem_limit_bytes=VMEM_LIMIT)
    hidden, leads, *kept = pl.pallas_call(
        first_kernel,
        name="first_half",
        out_shape=[
            pltpu.HBM(shape, bf16),
            jax.ShapeDtypeStruct((devices, slots, D + EXTRA), f32),
        ]
        + kept,
        in_specs=[scalars] * 2 + [anywhere] * 13,
        out_specs=[anywhere] + [vmem] * 7,
        scratch_shapes=[
            pltpu.VMEM((D, 3 * D), bf16),
            pltpu.VMEM((slots, D + EXTRA), f32),
            pltpu.VMEM((slots // TILES, half, D), bf16),
            pltpu.SMEM((slots // TILES * length // KEY_BLOCK + GROUP,), jnp.int32),
            pltpu.VMEM((2 * rows, D), bf16),
            pltpu.VMEM((2 * rows, D), bf16),
            pltpu.VMEM((2 * rows, D), bf16),
        ]
        + common
        + [dma((4,)), dma((slots,)), dma((TILES,)), dma((len(vectors),))],
        compiler_params=params,
        cost_estimate=cost,
    )(lengths, labels, *[in_hbm(a) for a in (sequences, qkv_weight, out_weight, up_weight, down_weight, *vectors)])
    gathered = lax.all_to_all(leads, AXES, 0, 0).reshape(devices * slots, D + EXTRA)
    hidden = pl.pallas_call(
        second_kernel,
        name="second_half",
        out_shape=pltpu.HBM(shape, bf16),
        in_specs=[vmem] * 6 + [anywhere],
        out_specs=anywhere,
        scratch_shapes=common + [dma((TILES,))],
        input_output_aliases={6: 0},
        compiler_params=params,
        cost_estimate=cost,
    )(*[pltpu.with_memory_space_constraint(a, pltpu.VMEM) for a in kept], in_hbm(hidden))
    one = lambda *shape: jax.ShapeDtypeStruct(shape, f32)
    logits, gpw, gpb, grw, grb, entropy = pl.pallas_call(
        ramp_kernel,
        name="off_ramp",
        out_shape=[one(CLASSES, slots), one(D, D), one(D), one(CLASSES, D), one(CLASSES), one(1, 1)],
        in_specs=[vmem] * 5,
        out_specs=[vmem] * 6,
        scratch_shapes=[pltpu.VMEM((devices * slots, CLASSES), f32)],
        compiler_params=params,
    )(gathered, pooler_weight, pooler_bias, ramp_weight.T, ramp_bias)
    return hidden.reshape(hidden_in.shape), logits.T, gpw, gpb, grw.T, grb, entropy.reshape(())


def solution(mesh):
    spread = P(AXES)
    placed = (P(AXES, None), spread, spread) + (P(),) * 16
    return jax.shard_map(
        local,
        mesh=mesh,
        in_specs=placed,
        out_specs=(P(AXES, None), P(AXES, None), P(), P(), P(), P(), P()),
        check_vma=False,
    )
```

```python
import functools

import jax
import jax.numpy as jnp
from jax import lax
from jax.experimental import pallas as pl
from jax.experimental.pallas import tpu as pltpu
from jax.sharding import PartitionSpec as P

D = 768
HEADS = 12
HEAD_DIM = 64
FF = 3072
CLASSES = 3
LANES = 128
KEY_BLOCK = 128
QUAD = 2 * LANES
GROUP = 4
EXTRA = 128
TILES = 2

AXES = ("wide", "narrow")
ROWS_BY_ROWS = (((1,), (1,)), ((), ()))
COLS_BY_COLS = (((0,), (0,)), ((), ()))
f32 = jnp.float32
bf16 = jnp.bfloat16


def product(left, right):
    return jnp.dot(left, right, preferred_element_type=f32)


def layer_norm(values, gain, shift):
    center = values - jnp.mean(values, axis=-1, keepdims=True)
    spread = jnp.mean(center * center, axis=-1, keepdims=True)
    return center * lax.rsqrt(spread + 1e-12) * gain + shift


def gelu(values):
    half = 0.5 * values
    return half + half * lax.erf(values * 0.7071067811865476)


def blocks_of(length):
    return (length + KEY_BLOCK - 1) // KEY_BLOCK


def project(tile, x, load_x, lengths, qkv_w, qkv_bias, table, queries, keys, values, keys_ready):
    slots, length = x.shape[0] // TILES, x.shape[1]
    per_slot = length // KEY_BLOCK

    def queries_step(step, carry):
        first = slots * tile + 2 * step
        for i in range(2):
            load_x(first + i).wait()
        tokens = x[pl.ds(first, 2)].reshape(2 * length, D)
        rows = pl.ds(pl.multiple_of(2 * length * step, 2 * length), 2 * length)
        for start in range(0, D, QUAD):
            lanes = slice(start, start + QUAD)
            found = (product(tokens, qkv_w[:, lanes]) + qkv_bias[:, lanes]).astype(bf16)
            queries[rows, lanes] = found * jnp.asarray(HEAD_DIM ** (-0.5), bf16)
        return carry

    lax.fori_loop(0, slots // 2, queries_step, 0)
    keys_ready()
    for entry in range(slots * per_slot + GROUP):
        table[entry] = 0
    total = 0
    for slot in range(slots):
        for block in range(per_slot):
            table[total + block] = slot * per_slot + block
        total = total + blocks_of(lengths[slots * tile + slot])

    def keys_step(group, carry):
        tokens = []
        for i in range(GROUP):
            entry = table[group * GROUP + i]
            row = pl.multiple_of(entry % per_slot * KEY_BLOCK, KEY_BLOCK)
            tokens.append(x[slots * tile + entry // per_slot, pl.ds(row, KEY_BLOCK), :])
        tokens = jnp.concatenate(tokens, axis=0)
        for kept, start in ((keys, D), (values, 2 * D)):
            lanes = slice(start, start + D)
            found = (product(tokens, qkv_w[:, lanes]) + qkv_bias[:, lanes]).astype(bf16)
            for i in range(GROUP):
                row = pl.multiple_of(table[group * GROUP + i] * KEY_BLOCK, KEY_BLOCK)
                kept[pl.ds(row, KEY_BLOCK), :] = found[i * KEY_BLOCK : (i + 1) * KEY_BLOCK]
        return carry

    lax.fori_loop(0, (total + GROUP - 1) // GROUP, keys_step, 0)


def attend(slot, blocks, length, queries, keys, values, contexts):
    low = lax.broadcasted_iota(jnp.int32, (1, LANES), 1) < HEAD_DIM
    zero = jnp.zeros((), bf16)
    half = contexts[0].shape[0]
    seen = blocks * KEY_BLOCK
    base = slot * 2 * half

    def apart(block):
        return jnp.concatenate([jnp.where(low, block, zero), jnp.where(low, zero, block)], axis=0)

    visible = seen - KEY_BLOCK + lax.broadcasted_iota(jnp.int32, (KEY_BLOCK, LANES), 0) < length
    ones = apart(jnp.ones((KEY_BLOCK, LANES), bf16))
    ones_last = apart(jnp.where(visible, 1.0, 0.0).astype(bf16))
    for pair in range(0, D, LANES):
        lanes = slice(pair, pair + LANES)
        key_blocks, value_blocks = [], []
        for start in range(0, seen, KEY_BLOCK):
            rows = pl.ds(pl.multiple_of(base + start, KEY_BLOCK), KEY_BLOCK)
            key_block, value_block, counted = keys[rows, lanes], values[rows, lanes], ones
            if start == 0:
                first_key = key_block[0:1, :]
            if start + KEY_BLOCK == seen:
                key_block = jnp.where(visible, key_block, first_key)
                value_block = jnp.where(visible, value_block, zero)
                counted = ones_last
            key_blocks.append(apart(key_block))
            value_blocks.append(jnp.concatenate([apart(value_block), counted], axis=1))
        for part, context in enumerate(contexts):
            rows = pl.ds(pl.multiple_of(base + part * half, half), half)
            mine = queries[rows, lanes]
            scores = [lax.dot_general(mine, block, ROWS_BY_ROWS, preferred_element_type=f32) for block in key_blocks]
            top = functools.reduce(jnp.maximum, scores)
            top_low = jnp.max(top[:, :KEY_BLOCK], axis=-1, keepdims=True)
            top_high = jnp.max(top[:, KEY_BLOCK:], axis=-1, keepdims=True)
            total = None
            for score, block in zip(scores, value_blocks):
                weights = jnp.concatenate(
                    [
                        jnp.exp(score[:, :KEY_BLOCK] - top_low).astype(bf16),
                        jnp.exp(score[:, KEY_BLOCK:] - top_high).astype(bf16),
                    ],
                    axis=1,
                )
                term = product(weights, block)
                total = term if total is None else total + term
            context[:, lanes] = (total[:, :LANES] / total[:, LANES:]).astype(bf16)


def close_attention(tile, first, x, context, out_w, vectors, after):
    out_bias, attention_gain, attention_shift = vectors
    per_tile, half = after.shape[0], after.shape[1]
    for j in range(per_tile):
        attended = product(context[j], out_w[...]) + out_bias
        tokens = x[per_tile * tile + j, first : first + half, :].astype(f32)
        after[j] = layer_norm(tokens + attended, attention_gain, attention_shift)


def feed_forward(tile, up_w, down_w, vectors, active, after, result, emit=None):
    up_bias, down_bias, output_gain, output_shift = vectors
    per_tile, half = after.shape[0], after.shape[1]
    total = per_tile * half
    for chunk in range(FF // D):
        spot = slice(chunk * D, (chunk + 1) * D)
        for j in range(0, per_tile, 2):
            rows = after[j : j + 2].reshape(2 * half, D).astype(bf16)
            expanded = product(rows, up_w[:, spot]) + up_bias[:, spot]
            active[chunk * total + j * half : chunk * total + (j + 2) * half, :] = gelu(expanded).astype(bf16)
    for j in range(per_tile):
        spread = [active[chunk * total + j * half : chunk * total + (j + 1) * half, :] for chunk in range(FF // D)]
        second = product(jnp.concatenate(spread, axis=1), down_w[...]) + down_bias
        done = layer_norm(after[j] + second, output_gain, output_shift).astype(bf16)
        result[tile, j] = done
        if emit is not None:
            emit(per_tile * tile + j, done)


def vectors_of(held):
    widths = (3 * D, D, D, D, FF, D, D, D)
    return [held[i : i + 1, :width] for i, width in enumerate(widths)]


def first_kernel(lengths, labels, x_hbm, qkv_hbm, out_hbm, up_hbm, down_hbm, *rest):
    vectors_hbm = rest[:8]
    hidden_hbm, later_hbm, leads_hbm = rest[8:11]
    x, later, out_w, up_w, down_w, held, qkv_w, lead, context, table, queries, keys, values, after, active, result, load_sem, x_sem, store_sem, vector_sem, later_sem, lead_sem = rest[11:]
    slots = x.shape[0]
    per_tile, half = result.shape[1:3]

    def load_x(slot):
        return pltpu.make_async_copy(x_hbm.at[slot], x.at[slot], x_sem.at[slot])

    sources = [(qkv_hbm.at[:, spot], qkv_w.at[:, spot]) for spot in (pl.ds(0, D), pl.ds(D, 2 * D))]
    sources += [(out_hbm, out_w), (up_hbm, up_w), (down_hbm, down_w)]
    loads = [pltpu.make_async_copy(a, b, load_sem.at[i]) for i, (a, b) in enumerate(sources)]
    small = [
        pltpu.make_async_copy(ref, held.at[i, pl.ds(0, ref.shape[0])], vector_sem.at[i])
        for i, ref in enumerate(vectors_hbm)
    ]
    for copy in (loads[0], load_x(0), load_x(1), *small):
        copy.start()

    def store(tile):
        return pltpu.make_async_copy(
            result.at[tile], hidden_hbm.at[pl.ds(per_tile * tile, per_tile), pl.ds(0, half), :], store_sem.at[tile]
        )

    def store_later(slot):
        return pltpu.make_async_copy(later.at[slot], later_hbm.at[slot], later_sem.at[slot])

    for copy in (loads[0], *small):
        copy.wait()
    loads[1].start()
    for slot in range(2, slots):
        load_x(slot).start()
    vectors = vectors_of(held)

    def attention_step(tile):
        def step(j, carry):
            slot = per_tile * tile + j
            for blocks in range(1, x.shape[1] // KEY_BLOCK + 1):

                @pl.when(blocks_of(lengths[slot]) == blocks)
                def _():
                    attend(j, blocks, lengths[slot], queries, keys, values, (context.at[j], later.at[slot]))

            store_later(slot).start()
            return carry

        return step

    def emit(slot, done):
        place = lax.broadcasted_iota(jnp.int32, (1, EXTRA), 1)
        facts = jnp.where(place == 0, lengths[slot], labels[slot]).astype(f32)
        lead[pl.ds(slot, 1), :] = jnp.concatenate([done[0:1, :].astype(f32), facts], axis=1)

    def tile_step(tile, carry):
        def keys_ready():
            @pl.when(tile == 0)
            def _():
                loads[1].wait()
                for load in loads[2:]:
                    load.start()

        project(tile, x, load_x, lengths, qkv_w, vectors[0], table, queries, keys, values, keys_ready)
        lax.fori_loop(0, per_tile, attention_step(tile), 0)

        @pl.when(tile == 0)
        def _():
            for load in loads[2:]:
                load.wait()

        close_attention(tile, 0, x, context, out_w, vectors[1:4], after)
        feed_forward(tile, up_w, down_w, vectors[4:], active, after, result, emit)
        store(tile).start()
        return carry

    lax.fori_loop(0, TILES, tile_step, 0)
    def each_device(act):
        def step(device, carry):
            act(pltpu.make_async_copy(lead, leads_hbm.at[device], lead_sem.at[device]))
            return carry

        lax.fori_loop(0, leads_hbm.shape[0], step, 0)

    each_device(lambda copy: copy.start())
    each_device(lambda copy: copy.wait())
    for tile in range(TILES):
        store(tile).wait()
    for slot in range(slots):
        store_later(slot).wait()


def second_kernel(x_hbm, context_hbm, out_hbm, up_hbm, down_hbm, *rest):
    vectors_hbm = rest[:8]
    hidden_in_place, hidden_hbm, x, context, out_w, up_w, down_w, held = rest[8:16]
    after, active, result, load_sem, x_sem, context_sem, store_sem, vector_sem = rest[16:]
    per_tile, half = result.shape[1:3]

    def load_rows(tile):
        spot = pl.ds(per_tile * tile, per_tile)
        return (
            pltpu.make_async_copy(context_hbm.at[spot], context.at[spot], context_sem.at[tile]),
            pltpu.make_async_copy(x_hbm.at[spot, pl.ds(half, half), :], x.at[spot], x_sem.at[tile]),
        )

    sources = [(out_hbm, out_w), (up_hbm, up_w), (down_hbm, down_w)]
    loads = [pltpu.make_async_copy(a, b, load_sem.at[i]) for i, (a, b) in enumerate(sources)]
    small = [
        pltpu.make_async_copy(ref, held.at[i, pl.ds(0, ref.shape[0])], vector_sem.at[i])
        for i, ref in enumerate(vectors_hbm)
    ]
    for copy in (loads[0], *load_rows(0), *small):
        copy.start()
    for copy in (loads[0], *load_rows(0), *small):
        copy.wait()
    for tile in range(1, TILES):
        for copy in load_rows(tile):
            copy.start()
    for load in loads[1:]:
        load.start()
    vectors = vectors_of(held)

    def store(tile):
        return pltpu.make_async_copy(
            result.at[tile], hidden_hbm.at[pl.ds(per_tile * tile, per_tile), pl.ds(half, half), :], store_sem.at[tile]
        )

    def attention_step(tile, carry):
        @pl.when(tile > 0)
        def _():
            for copy in load_rows(tile):
                copy.wait()

        mine = pl.ds(per_tile * tile, per_tile)
        close_attention(tile, 0, x, context.at[mine], out_w, vectors[1:4], after.at[mine])
        return carry

    def tile_step(tile, carry):
        mine = pl.ds(per_tile * tile, per_tile)
        feed_forward(tile, up_w, down_w, vectors[4:], active, after.at[mine], result)
        store(tile).start()
        return carry

    lax.fori_loop(0, TILES, attention_step, 0)
    for load in loads[1:]:
        load.wait()
    lax.fori_loop(0, TILES, tile_step, 0)
    for tile in range(TILES):
        store(tile).wait()


def ramp_kernel(gathered, pooler_w, pooler_b, ramp_t, ramp_b, logits_out, gpw_out, gpb_out, grw_out, grb_out, entropy_out, scored, found, sem):
    own = logits_out.shape[1]
    leading = gathered[:, :D].astype(bf16)
    lengths = gathered[:, D : D + 1]
    labels = gathered[:, D + 1 : D + 2]
    pooled = jnp.tanh(product(leading, pooler_w[...]) + pooler_b[...].reshape(1, -1))
    ramp = [ramp_t[c : c + 1, :] for c in range(CLASSES)]
    bias = ramp_b[...].reshape(1, -1)
    logits = [jnp.sum(pooled * ramp[c], axis=1, keepdims=True) + bias[:, c : c + 1] for c in range(CLASSES)]
    scored[...] = jnp.concatenate(logits, axis=1)
    wide, narrow = lax.axis_index(AXES[0]), lax.axis_index(AXES[1])
    place = wide * lax.axis_size(AXES[1]) + narrow
    logits_out[...] = scored[pl.ds(pl.multiple_of(place * own, own), own), :].T
    top = functools.reduce(jnp.maximum, logits)
    shifted = [one - top for one in logits]
    powers = [jnp.exp(one) for one in shifted]
    total = sum(powers[1:], powers[0])
    dlogits = [powers[c] / total - jnp.where(labels == float(c), 1.0, 0.0) for c in range(CLASSES)]
    back = sum((dlogits[c] * ramp[c] for c in range(1, CLASSES)), dlogits[0] * ramp[0])
    pooled_grad = (back * (1.0 - pooled * pooled)).astype(bf16)
    copies = []
    for i in range(D // QUAD):
        rows = slice(i * QUAD, (i + 1) * QUAD)
        found[rows, :] = lax.dot_general(leading[:, rows], pooled_grad, COLS_BY_COLS, preferred_element_type=f32)
        copies.append(pltpu.make_async_copy(found.at[rows], gpw_out.at[rows], sem.at[i]))
        copies[i].start()
    gpb_out[...] = jnp.sum(pooled_grad.astype(f32), axis=0)
    for c in range(CLASSES):
        grw_out[c : c + 1, :] = jnp.sum(pooled * dlogits[c], axis=0, keepdims=True)
    grb_out[...] = jnp.concatenate([jnp.sum(one, axis=0) for one in dlogits])
    log_total = jnp.log(total)
    log_probs = [one - log_total for one in shifted]
    row_entropy = -sum((jnp.exp(one) * one for one in log_probs[1:]), jnp.exp(log_probs[0]) * log_probs[0])
    entropy_out[...] = jnp.sum(lengths * row_entropy, axis=0, keepdims=True) / jnp.sum(lengths, axis=0, keepdims=True)
    for copy in copies:
        copy.wait()


VMEM_LIMIT = 56 * 1024 * 1024
SECOND_LIMIT = 48 * 1024 * 1024


def local(
    hidden_in, lengths, labels,
    qkv_weight, qkv_bias, out_weight, out_bias, attention_gain, attention_shift,
    up_weight, up_bias, down_weight, down_bias, output_gain, output_shift,
    pooler_weight, pooler_bias, ramp_weight, ramp_bias,
):
    slots = lengths.shape[0]
    length = hidden_in.shape[0] // slots
    half = length // 2
    rows = slots // TILES * half
    shape = (slots, length, D)
    devices = lax.axis_size(AXES)
    sequences = hidden_in.reshape(shape)
    vectors = (qkv_bias, out_bias, attention_gain, attention_shift, up_bias, down_bias, output_gain, output_shift)
    anywhere = pl.BlockSpec(memory_space=pltpu.HBM)
    in_hbm = lambda array: pltpu.with_memory_space_constraint(array, pltpu.HBM)
    scalars = pl.BlockSpec(memory_space=pltpu.SMEM)
    vmem = pl.BlockSpec(memory_space=pltpu.VMEM)
    dma = pltpu.SemaphoreType.DMA
    weights = [pltpu.VMEM(one, bf16) for one in ((D, D), (D, FF), (FF, D))]
    weights = weights + [pltpu.VMEM((len(vectors), FF), f32)]
    common = [
        pltpu.VMEM((rows * FF // D, D), bf16),
        pltpu.VMEM((TILES, slots // TILES, half, D), bf16),
    ]
    cost = pl.CostEstimate(
        flops=2 * slots * half * D * (2 * D + 2 * FF + 2 * length), bytes_accessed=30_000_000, transcendentals=0
    )
    params = pltpu.CompilerParams(vmem_limit_bytes=VMEM_LIMIT)
    hidden, later, leads = pl.pallas_call(
        first_kernel,
        name="first_half",
        out_shape=[
            pltpu.HBM(shape, bf16),
            pltpu.HBM((slots, half, D), bf16),
            pltpu.HBM((devices, slots, D + EXTRA), f32),
        ],
        in_specs=[scalars] * 2 + [anywhere] * 13,
        out_specs=[anywhere] * 3,
        scratch_shapes=[pltpu.VMEM(shape, bf16), pltpu.VMEM((slots, half, D), bf16)]
        + weights
        + [
            pltpu.VMEM((D, 3 * D), bf16),
            pltpu.VMEM((slots, D + EXTRA), f32),
            pltpu.VMEM((slots // TILES, half, D), bf16),
            pltpu.SMEM((slots // TILES * length // KEY_BLOCK + GROUP,), jnp.int32),
            pltpu.VMEM((2 * rows, D), bf16),
            pltpu.VMEM((2 * rows, D), bf16),
            pltpu.VMEM((2 * rows, D), bf16),
        ]
        + [pltpu.VMEM((slots // TILES, half, D), f32)]
        + common
        + [dma((5,)), dma((slots,)), dma((TILES,)), dma((len(vectors),)), dma((slots,)), dma((devices,))],
        compiler_params=params,
        cost_estimate=cost,
    )(lengths, labels, *[in_hbm(a) for a in (sequences, qkv_weight, out_weight, up_weight, down_weight, *vectors)])
    gathered = lax.all_to_all(leads, AXES, 0, 0).reshape(devices * slots, D + EXTRA)
    hidden = pl.pallas_call(
        second_kernel,
        name="second_half",
        out_shape=pltpu.HBM(shape, bf16),
        in_specs=[anywhere] * 14,
        out_specs=anywhere,
        scratch_shapes=[pltpu.VMEM((slots, half, D), bf16)] * 2
        + weights
        + [pltpu.VMEM((slots, half, D), f32)]
        + common
        + [dma((3,)), dma((TILES,)), dma((TILES,)), dma((TILES,)), dma((len(vectors),))],
        input_output_aliases={13: 0},
        compiler_params=pltpu.CompilerParams(vmem_limit_bytes=SECOND_LIMIT),
        cost_estimate=cost,
    )(*[in_hbm(a) for a in (sequences, later, out_weight, up_weight, down_weight, *vectors, hidden)])
    one = lambda *shape: jax.ShapeDtypeStruct(shape, f32)
    logits, gpw, gpb, grw, grb, entropy = pl.pallas_call(
        ramp_kernel,
        name="off_ramp",
        out_shape=[one(CLASSES, slots), pltpu.HBM((D, D), f32), one(D), one(CLASSES, D), one(CLASSES), one(1, 1)],
        in_specs=[vmem] * 5,
        out_specs=[vmem, anywhere] + [vmem] * 4,
        scratch_shapes=[pltpu.VMEM((devices * slots, CLASSES), f32), pltpu.VMEM((D, D), f32), dma((D // QUAD,))],
        compiler_params=params,
    )(gathered, pooler_weight, pooler_bias, ramp_weight.T, ramp_bias)
    return hidden.reshape(hidden_in.shape), logits.T, gpw, gpb, grw.T, grb, entropy.reshape(())


def solution(mesh):
    spread = P(AXES)
    placed = (P(AXES, None), spread, spread) + (P(),) * 16
    return jax.shard_map(
        local,
        mesh=mesh,
        in_specs=placed,
        out_specs=(P(AXES, None), P(AXES, None), P(), P(), P(), P(), P()),
        check_vma=False,
    )
```

```python
import functools

import jax
import jax.numpy as jnp
from jax import lax
from jax.experimental import pallas as pl
from jax.experimental.pallas import tpu as pltpu
from jax.sharding import PartitionSpec as P

D = 768
HEADS = 12
HEAD_DIM = 64
FF = 3072
CLASSES = 3
LANES = 128
KEY_BLOCK = 128
QUAD = 2 * LANES
GROUP = 4
EXTRA = 128
SAFE = 1e25
TILES = 2

AXES = ("wide", "narrow")
ROWS_BY_ROWS = (((1,), (1,)), ((), ()))
COLS_BY_COLS = (((0,), (0,)), ((), ()))
f32 = jnp.float32
bf16 = jnp.bfloat16


def product(left, right):
    return jnp.dot(left, right, preferred_element_type=f32)


def layer_norm(values, gain, shift):
    center = values - jnp.mean(values, axis=-1, keepdims=True)
    spread = jnp.mean(center * center, axis=-1, keepdims=True)
    return center * lax.rsqrt(spread + 1e-12) * gain + shift


def gelu(values):
    half = 0.5 * values
    return half + half * lax.erf(values * 0.7071067811865476)


def blocks_of(length):
    return (length + KEY_BLOCK - 1) // KEY_BLOCK


def project(tile, x, load_x, lengths, qkv_w, qkv_bias, table, queries, keys, values, keys_ready):
    slots, length = x.shape[0] // TILES, x.shape[1]
    per_slot = length // KEY_BLOCK

    def queries_step(step, carry):
        first = slots * tile + 2 * step
        for i in range(2):
            load_x(first + i).wait()
        tokens = x[pl.ds(first, 2)].reshape(2 * length, D)
        rows = pl.ds(pl.multiple_of(2 * length * step, 2 * length), 2 * length)
        for start in range(0, D, QUAD):
            lanes = slice(start, start + QUAD)
            found = (product(tokens, qkv_w[:, lanes]) + qkv_bias[:, lanes]).astype(bf16)
            queries[rows, lanes] = found * jnp.asarray(HEAD_DIM ** (-0.5), bf16)
        return carry

    lax.fori_loop(0, slots // 2, queries_step, 0)
    keys_ready()
    for entry in range(slots * per_slot + GROUP):
        table[entry] = 0
    total = 0
    for slot in range(slots):
        for block in range(per_slot):
            table[total + block] = slot * per_slot + block
        total = total + blocks_of(lengths[slots * tile + slot])

    def keys_step(group, carry):
        tokens = []
        for i in range(GROUP):
            entry = table[group * GROUP + i]
            row = pl.multiple_of(entry % per_slot * KEY_BLOCK, KEY_BLOCK)
            tokens.append(x[slots * tile + entry // per_slot, pl.ds(row, KEY_BLOCK), :])
        tokens = jnp.concatenate(tokens, axis=0)
        for kept, start in ((keys, D), (values, 2 * D)):
            lanes = slice(start, start + D)
            found = (product(tokens, qkv_w[:, lanes]) + qkv_bias[:, lanes]).astype(bf16)
            for i in range(GROUP):
                row = pl.multiple_of(table[group * GROUP + i] * KEY_BLOCK, KEY_BLOCK)
                kept[pl.ds(row, KEY_BLOCK), :] = found[i * KEY_BLOCK : (i + 1) * KEY_BLOCK]
        return carry

    lax.fori_loop(0, (total + GROUP - 1) // GROUP, keys_step, 0)


def two_heads(low, block):
    zero = jnp.zeros((), block.dtype)
    return jnp.concatenate([jnp.where(low, block, zero), jnp.where(low, zero, block)], axis=0)


def visible_rows(start, length):
    return start + lax.broadcasted_iota(jnp.int32, (KEY_BLOCK, LANES), 0) < length


def attend(slot, blocks, length, queries, keys, values, contexts, extremes):
    low = lax.broadcasted_iota(jnp.int32, (1, LANES), 1) < HEAD_DIM
    half = contexts[0].shape[0]
    seen = blocks * KEY_BLOCK
    base = slot * 2 * half
    visible = visible_rows(seen - KEY_BLOCK, length)
    ones = two_heads(low, jnp.ones((KEY_BLOCK, LANES), bf16))
    ones_last = two_heads(low, jnp.where(visible, 1.0, 0.0).astype(bf16))
    extreme = None
    for pair in range(0, D, LANES):
        lanes = slice(pair, pair + LANES)
        key_blocks, value_blocks = [], []
        for start in range(0, seen, KEY_BLOCK):
            rows = pl.ds(pl.multiple_of(base + start, KEY_BLOCK), KEY_BLOCK)
            value_block, counted = values[rows, lanes], ones
            if start + KEY_BLOCK == seen:
                value_block = jnp.where(visible, value_block, jnp.zeros((), bf16))
                counted = ones_last
            key_blocks.append(two_heads(low, keys[rows, lanes]))
            value_blocks.append(jnp.concatenate([two_heads(low, value_block), counted], axis=1))
        for part, context in enumerate(contexts):
            rows = pl.ds(pl.multiple_of(base + part * half, half), half)
            mine = queries[rows, lanes]
            total = None
            for key_block, value_block in zip(key_blocks, value_blocks):
                scores = lax.dot_general(mine, key_block, ROWS_BY_ROWS, preferred_element_type=f32)
                term = product(jnp.exp(scores).astype(bf16), value_block)
                total = term if total is None else total + term
            sums = total[:, LANES:]
            inverse = 1.0 / sums
            context[:, lanes] = (total[:, :LANES] * inverse).astype(bf16)
            farthest = jnp.max(jnp.maximum(sums, inverse).reshape(half // 8, 8, LANES), axis=0)
            extreme = farthest if extreme is None else jnp.maximum(extreme, farthest)
    extremes[...] = extreme


def attend_shifted(slot, length, queries, keys, values, contexts):
    low = lax.broadcasted_iota(jnp.int32, (1, LANES), 1) < HEAD_DIM
    half = contexts[0].shape[0]
    base = slot * 2 * half

    def pair_step(pair, carry):
        lanes = pl.ds(pl.multiple_of(pair * LANES, LANES), LANES)
        key_blocks, value_blocks = [], []
        for start in range(0, 2 * half, KEY_BLOCK):
            rows = pl.ds(pl.multiple_of(base + start, KEY_BLOCK), KEY_BLOCK)
            visible = visible_rows(start, length)
            key_block, value_block = keys[rows, lanes], values[rows, lanes]
            if start == 0:
                first_key = key_block[0:1, :]
            key_blocks.append(two_heads(low, jnp.where(visible, key_block, first_key)))
            value_block = jnp.where(visible, value_block, jnp.zeros((), bf16))
            counted = jnp.where(visible, 1.0, 0.0).astype(bf16)
            value_blocks.append(jnp.concatenate([two_heads(low, value_block), two_heads(low, counted)], axis=1))

        def rows_step(context, start, step):
            offset = pl.multiple_of(step * KEY_BLOCK, KEY_BLOCK)
            mine = queries[pl.ds(pl.multiple_of(base + start + offset, KEY_BLOCK), KEY_BLOCK), lanes]
            scores = [lax.dot_general(mine, block, ROWS_BY_ROWS, preferred_element_type=f32) for block in key_blocks]
            top = functools.reduce(jnp.maximum, scores)
            top_low = jnp.max(top[:, :KEY_BLOCK], axis=-1, keepdims=True)
            top_high = jnp.max(top[:, KEY_BLOCK:], axis=-1, keepdims=True)
            total = None
            for score, block in zip(scores, value_blocks):
                shifted = jnp.concatenate([score[:, :KEY_BLOCK] - top_low, score[:, KEY_BLOCK:] - top_high], axis=1)
                term = product(jnp.exp(shifted).astype(bf16), block)
                total = term if total is None else total + term
            context[pl.ds(offset, KEY_BLOCK), lanes] = (total[:, :LANES] / total[:, LANES:]).astype(bf16)

        for part, context in enumerate(contexts):

            def step(i, carry, part=part, context=context):
                rows_step(context, part * half, i)
                return carry

            lax.fori_loop(0, half // KEY_BLOCK, step, 0)
        return carry

    lax.fori_loop(0, D // LANES, pair_step, 0)


def close_attention(slot, first, x, context, out_w, vectors, after):
    out_bias, attention_gain, attention_shift = vectors
    slots, half = after.shape[0], after.shape[1]
    for j in range(slots):
        attended = product(context[j], out_w[...]) + out_bias
        tokens = x[slot + j, first : first + half, :].astype(f32)
        after[j] = layer_norm(tokens + attended, attention_gain, attention_shift)


def feed_forward(tile, up_w, down_w, vectors, active, after, result, emit=None):
    up_bias, down_bias, output_gain, output_shift = vectors
    per_tile, half = after.shape[0], after.shape[1]
    total = per_tile * half
    for chunk in range(FF // D):
        spot = slice(chunk * D, (chunk + 1) * D)
        for j in range(0, per_tile, 2):
            rows = after[j : j + 2].reshape(2 * half, D).astype(bf16)
            expanded = product(rows, up_w[:, spot]) + up_bias[:, spot]
            active[chunk * total + j * half : chunk * total + (j + 2) * half, :] = gelu(expanded).astype(bf16)
    for j in range(per_tile):
        spread = [active[chunk * total + j * half : chunk * total + (j + 1) * half, :] for chunk in range(FF // D)]
        second = product(jnp.concatenate(spread, axis=1), down_w[...]) + down_bias
        done = layer_norm(after[j] + second, output_gain, output_shift).astype(bf16)
        result[tile, j] = done
        if emit is not None:
            emit(per_tile * tile + j, done)


def vectors_of(held):
    widths = (3 * D, D, D, D, FF, D, D, D)
    return [held[i : i + 1, :width] for i, width in enumerate(widths)]


def first_kernel(lengths, labels, x_hbm, qkv_hbm, out_hbm, up_hbm, down_hbm, *rest):
    vectors_hbm = rest[:8]
    hidden_hbm, later_hbm, leads_hbm = rest[8:11]
    x, later, out_w, up_w, down_w, held, qkv_w, lead, context, table, queries, keys, values, extremes, after, active, result, load_sem, x_sem, store_sem, vector_sem, later_sem, lead_sem = rest[11:]
    slots = x.shape[0]
    per_tile, half = result.shape[1:3]

    def load_x(slot):
        return pltpu.make_async_copy(x_hbm.at[slot], x.at[slot], x_sem.at[slot])

    sources = [(qkv_hbm.at[:, spot], qkv_w.at[:, spot]) for spot in (pl.ds(0, D), pl.ds(D, 2 * D))]
    sources += [(out_hbm, out_w), (up_hbm, up_w), (down_hbm, down_w)]
    loads = [pltpu.make_async_copy(a, b, load_sem.at[i]) for i, (a, b) in enumerate(sources)]
    small = [
        pltpu.make_async_copy(ref, held.at[i, pl.ds(0, ref.shape[0])], vector_sem.at[i])
        for i, ref in enumerate(vectors_hbm)
    ]
    for copy in (loads[0], load_x(0), load_x(1), *small):
        copy.start()

    def store(tile):
        return pltpu.make_async_copy(
            result.at[tile], hidden_hbm.at[pl.ds(per_tile * tile, per_tile), pl.ds(0, half), :], store_sem.at[tile]
        )

    def store_later(slot):
        return pltpu.make_async_copy(later.at[slot], later_hbm.at[slot], later_sem.at[slot])

    for copy in (loads[0], *small):
        copy.wait()
    loads[1].start()
    for slot in range(2, slots):
        load_x(slot).start()
    vectors = vectors_of(held)

    def contexts_of(tile, j):
        return context.at[j], later.at[per_tile * tile + j]

    def attention_step(tile):
        def step(j, carry):
            length = lengths[per_tile * tile + j]
            for blocks in range(1, x.shape[1] // KEY_BLOCK + 1):

                @pl.when(blocks_of(length) == blocks)
                def _():
                    attend(j, blocks, length, queries, keys, values, contexts_of(tile, j), extremes.at[j])

            return carry

        return step

    def shifted_step(tile):
        def step(j, carry):
            length = lengths[per_tile * tile + j]
            attend_shifted(j, length, queries, keys, values, contexts_of(tile, j))
            return carry

        return step

    def emit(slot, done):
        place = lax.broadcasted_iota(jnp.int32, (1, EXTRA), 1)
        facts = jnp.where(place == 0, lengths[slot], labels[slot]).astype(f32)
        lead[pl.ds(slot, 1), :] = jnp.concatenate([done[0:1, :].astype(f32), facts], axis=1)

    def tile_step(tile, carry):
        def keys_ready():
            @pl.when(tile == 0)
            def _():
                loads[1].wait()
                for load in loads[2:]:
                    load.start()

        project(tile, x, load_x, lengths, qkv_w, vectors[0], table, queries, keys, values, keys_ready)
        lax.fori_loop(0, per_tile, attention_step(tile), 0)

        @pl.when(jnp.logical_not(jnp.max(extremes[...]) <= SAFE))
        def _():
            lax.fori_loop(0, per_tile, shifted_step(tile), 0)

        for j in range(per_tile):
            store_later(per_tile * tile + j).start()

        @pl.when(tile == 0)
        def _():
            for load in loads[2:]:
                load.wait()

        close_attention(per_tile * tile, 0, x, context, out_w, vectors[1:4], after)
        feed_forward(tile, up_w, down_w, vectors[4:], active, after, result, emit)
        store(tile).start()
        return carry

    lax.fori_loop(0, TILES, tile_step, 0)
    def each_device(act):
        def step(device, carry):
            act(pltpu.make_async_copy(lead, leads_hbm.at[device], lead_sem.at[device]))
            return carry

        lax.fori_loop(0, leads_hbm.shape[0], step, 0)

    each_device(lambda copy: copy.start())
    each_device(lambda copy: copy.wait())
    for tile in range(TILES):
        store(tile).wait()
    for slot in range(slots):
        store_later(slot).wait()


def second_kernel(x_hbm, context_hbm, out_hbm, up_hbm, down_hbm, *rest):
    vectors_hbm = rest[:8]
    hidden_in_place, hidden_hbm, x, context, out_w, up_w, down_w, held = rest[8:16]
    after, active, result, load_sem, x_sem, context_sem, store_sem, vector_sem = rest[16:]
    per_tile, half = result.shape[1:3]

    def load_rows(tile):
        spot = pl.ds(per_tile * tile, per_tile)
        return (
            pltpu.make_async_copy(context_hbm.at[spot], context.at[spot], context_sem.at[tile]),
            pltpu.make_async_copy(x_hbm.at[spot, pl.ds(half, half), :], x.at[spot], x_sem.at[tile]),
        )

    sources = [(out_hbm, out_w), (up_hbm, up_w), (down_hbm, down_w)]
    loads = [pltpu.make_async_copy(a, b, load_sem.at[i]) for i, (a, b) in enumerate(sources)]
    small = [
        pltpu.make_async_copy(ref, held.at[i, pl.ds(0, ref.shape[0])], vector_sem.at[i])
        for i, ref in enumerate(vectors_hbm)
    ]
    for copy in (loads[0], *load_rows(0), *small):
        copy.start()
    for copy in (loads[0], *load_rows(0), *small):
        copy.wait()
    for tile in range(1, TILES):
        for copy in load_rows(tile):
            copy.start()
    for load in loads[1:]:
        load.start()
    vectors = vectors_of(held)

    def store(tile):
        return pltpu.make_async_copy(
            result.at[tile], hidden_hbm.at[pl.ds(per_tile * tile, per_tile), pl.ds(half, half), :], store_sem.at[tile]
        )

    def attention_step(step, carry):
        @pl.when(step == per_tile // 2)
        def _():
            for tile in range(1, TILES):
                for copy in load_rows(tile):
                    copy.wait()

        mine = pl.ds(2 * step, 2)
        close_attention(2 * step, 0, x, context.at[mine], out_w, vectors[1:4], after.at[mine])
        return carry

    def tile_step(tile, carry):
        mine = pl.ds(per_tile * tile, per_tile)
        feed_forward(tile, up_w, down_w, vectors[4:], active, after.at[mine], result)
        store(tile).start()
        return carry

    lax.fori_loop(0, x.shape[0] // 2, attention_step, 0)
    for load in loads[1:]:
        load.wait()
    lax.fori_loop(0, TILES, tile_step, 0)
    for tile in range(TILES):
        store(tile).wait()


def ramp_kernel(gathered, pooler_w, pooler_b, ramp_t, ramp_b, logits_out, gpw_out, gpb_out, grw_out, grb_out, entropy_out, scored, found, sem):
    own = logits_out.shape[1]
    leading = gathered[:, :D].astype(bf16)
    lengths = gathered[:, D : D + 1]
    labels = gathered[:, D + 1 : D + 2]
    pooled = jnp.tanh(product(leading, pooler_w[...]) + pooler_b[...].reshape(1, -1))
    ramp = [ramp_t[c : c + 1, :] for c in range(CLASSES)]
    bias = ramp_b[...].reshape(1, -1)
    logits = [jnp.sum(pooled * ramp[c], axis=1, keepdims=True) + bias[:, c : c + 1] for c in range(CLASSES)]
    scored[...] = jnp.concatenate(logits, axis=1)
    wide, narrow = lax.axis_index(AXES[0]), lax.axis_index(AXES[1])
    place = wide * lax.axis_size(AXES[1]) + narrow
    logits_out[...] = scored[pl.ds(pl.multiple_of(place * own, own), own), :].T
    top = functools.reduce(jnp.maximum, logits)
    shifted = [one - top for one in logits]
    powers = [jnp.exp(one) for one in shifted]
    total = sum(powers[1:], powers[0])
    dlogits = [powers[c] / total - jnp.where(labels == float(c), 1.0, 0.0) for c in range(CLASSES)]
    back = sum((dlogits[c] * ramp[c] for c in range(1, CLASSES)), dlogits[0] * ramp[0])
    pooled_grad = (back * (1.0 - pooled * pooled)).astype(bf16)
    copies = []
    for i in range(D // QUAD):
        rows = slice(i * QUAD, (i + 1) * QUAD)
        found[rows, :] = lax.dot_general(leading[:, rows], pooled_grad, COLS_BY_COLS, preferred_element_type=f32)
        copies.append(pltpu.make_async_copy(found.at[rows], gpw_out.at[rows], sem.at[i]))
        copies[i].start()
    gpb_out[...] = jnp.sum(pooled_grad.astype(f32), axis=0)
    for c in range(CLASSES):
        grw_out[c : c + 1, :] = jnp.sum(pooled * dlogits[c], axis=0, keepdims=True)
    grb_out[...] = jnp.concatenate([jnp.sum(one, axis=0) for one in dlogits])
    log_total = jnp.log(total)
    log_probs = [one - log_total for one in shifted]
    row_entropy = -sum((jnp.exp(one) * one for one in log_probs[1:]), jnp.exp(log_probs[0]) * log_probs[0])
    entropy_out[...] = jnp.sum(lengths * row_entropy, axis=0, keepdims=True) / jnp.sum(lengths, axis=0, keepdims=True)
    for copy in copies:
        copy.wait()


VMEM_LIMIT = 56 * 1024 * 1024
SECOND_LIMIT = 42 * 1024 * 1024


def local(
    hidden_in, lengths, labels,
    qkv_weight, qkv_bias, out_weight, out_bias, attention_gain, attention_shift,
    up_weight, up_bias, down_weight, down_bias, output_gain, output_shift,
    pooler_weight, pooler_bias, ramp_weight, ramp_bias,
):
    slots = lengths.shape[0]
    length = hidden_in.shape[0] // slots
    half = length // 2
    rows = slots // TILES * half
    shape = (slots, length, D)
    devices = lax.axis_size(AXES)
    sequences = hidden_in.reshape(shape)
    vectors = (qkv_bias, out_bias, attention_gain, attention_shift, up_bias, down_bias, output_gain, output_shift)
    anywhere = pl.BlockSpec(memory_space=pltpu.HBM)
    in_hbm = lambda array: pltpu.with_memory_space_constraint(array, pltpu.HBM)
    scalars = pl.BlockSpec(memory_space=pltpu.SMEM)
    vmem = pl.BlockSpec(memory_space=pltpu.VMEM)
    dma = pltpu.SemaphoreType.DMA
    weights = [pltpu.VMEM(one, bf16) for one in ((D, D), (D, FF), (FF, D))]
    weights = weights + [pltpu.VMEM((len(vectors), FF), f32)]
    common = [
        pltpu.VMEM((rows * FF // D, D), bf16),
        pltpu.VMEM((TILES, slots // TILES, half, D), bf16),
    ]
    cost = pl.CostEstimate(
        flops=2 * slots * half * D * (2 * D + 2 * FF + 2 * length), bytes_accessed=30_000_000, transcendentals=0
    )
    params = pltpu.CompilerParams(vmem_limit_bytes=VMEM_LIMIT)
    hidden, later, leads = pl.pallas_call(
        first_kernel,
        name="first_half",
        out_shape=[
            pltpu.HBM(shape, bf16),
            pltpu.HBM((slots, half, D), bf16),
            pltpu.HBM((devices, slots, D + EXTRA), f32),
        ],
        in_specs=[scalars] * 2 + [anywhere] * 13,
        out_specs=[anywhere] * 3,
        scratch_shapes=[pltpu.VMEM(shape, bf16), pltpu.VMEM((slots, half, D), bf16)]
        + weights
        + [
            pltpu.VMEM((D, 3 * D), bf16),
            pltpu.VMEM((slots, D + EXTRA), f32),
            pltpu.VMEM((slots // TILES, half, D), bf16),
            pltpu.SMEM((slots // TILES * length // KEY_BLOCK + GROUP,), jnp.int32),
            pltpu.VMEM((2 * rows, D), bf16),
            pltpu.VMEM((2 * rows, D), bf16),
            pltpu.VMEM((2 * rows, D), bf16),
            pltpu.VMEM((slots // TILES, 8, LANES), f32),
        ]
        + [pltpu.VMEM((slots // TILES, half, D), f32)]
        + common
        + [dma((5,)), dma((slots,)), dma((TILES,)), dma((len(vectors),)), dma((slots,)), dma((devices,))],
        compiler_params=params,
        cost_estimate=cost,
    )(lengths, labels, *[in_hbm(a) for a in (sequences, qkv_weight, out_weight, up_weight, down_weight, *vectors)])
    gathered = lax.all_to_all(leads, AXES, 0, 0).reshape(devices * slots, D + EXTRA)
    hidden = pl.pallas_call(
        second_kernel,
        name="second_half",
        out_shape=pltpu.HBM(shape, bf16),
        in_specs=[anywhere] * 14,
        out_specs=anywhere,
        scratch_shapes=[pltpu.VMEM((slots, half, D), bf16)] * 2
        + weights
        + [pltpu.VMEM((slots, half, D), f32)]
        + common
        + [dma((3,)), dma((TILES,)), dma((TILES,)), dma((TILES,)), dma((len(vectors),))],
        input_output_aliases={13: 0},
        compiler_params=pltpu.CompilerParams(vmem_limit_bytes=SECOND_LIMIT),
        cost_estimate=cost,
    )(*[in_hbm(a) for a in (sequences, later, out_weight, up_weight, down_weight, *vectors, hidden)])
    one = lambda *shape: jax.ShapeDtypeStruct(shape, f32)
    logits, gpw, gpb, grw, grb, entropy = pl.pallas_call(
        ramp_kernel,
        name="off_ramp",
        out_shape=[one(CLASSES, slots), pltpu.HBM((D, D), f32), one(D), one(CLASSES, D), one(CLASSES), one(1, 1)],
        in_specs=[vmem] * 5,
        out_specs=[vmem, anywhere] + [vmem] * 4,
        scratch_shapes=[pltpu.VMEM((devices * slots, CLASSES), f32), pltpu.VMEM((D, D), f32), dma((D // QUAD,))],
        compiler_params=pltpu.CompilerParams(vmem_limit_bytes=8 * 1024 * 1024 + 5 * 4 * gathered.size),
    )(gathered, pooler_weight, pooler_bias, ramp_weight.T, ramp_bias)
    return hidden.reshape(hidden_in.shape), logits.T, gpw, gpb, grw.T, grb, entropy.reshape(())


def solution(mesh):
    spread = P(AXES)
    placed = (P(AXES, None), spread, spread) + (P(),) * 16
    return jax.shard_map(
        local,
        mesh=mesh,
        in_specs=placed,
        out_specs=(P(AXES, None), P(AXES, None), P(), P(), P(), P(), P()),
        check_vma=False,
    )
```

```python
import functools

import jax
import jax.numpy as jnp
from jax import lax
from jax.experimental import pallas as pl
from jax.experimental.pallas import tpu as pltpu
from jax.sharding import PartitionSpec as P

D = 768
HEADS = 12
HEAD_DIM = 64
FF = 3072
CLASSES = 3
LANES = 128
KEY_BLOCK = 128
QUAD = 2 * LANES
GROUP = 4
EXTRA = 128
SAFE = 1e25
TILES = 2

AXES = ("wide", "narrow")
ROWS_BY_ROWS = (((1,), (1,)), ((), ()))
COLS_BY_COLS = (((0,), (0,)), ((), ()))
f32 = jnp.float32
bf16 = jnp.bfloat16


def product(left, right):
    return jnp.dot(left, right, preferred_element_type=f32)


def layer_norm(values, gain, shift):
    center = values - jnp.mean(values, axis=-1, keepdims=True)
    spread = jnp.mean(center * center, axis=-1, keepdims=True)
    return center * lax.rsqrt(spread + 1e-12) * gain + shift


def gelu(values):
    half = 0.5 * values
    return half + half * lax.erf(values * 0.7071067811865476)


def blocks_of(length):
    return (length + KEY_BLOCK - 1) // KEY_BLOCK


def project(tile, x, load_x, lengths, qkv_w, qkv_bias, table, queries, keys, values, keys_ready):
    slots, length = x.shape[0] // TILES, x.shape[1]
    per_slot = length // KEY_BLOCK

    def queries_step(step, carry):
        first = slots * tile + 2 * step
        for i in range(2):
            load_x(first + i).wait()
        tokens = x[pl.ds(first, 2)].reshape(2 * length, D)
        rows = pl.ds(pl.multiple_of(2 * length * step, 2 * length), 2 * length)
        for start in range(0, D, QUAD):
            lanes = slice(start, start + QUAD)
            found = (product(tokens, qkv_w[:, lanes]) + qkv_bias[:, lanes]).astype(bf16)
            queries[rows, lanes] = found * jnp.asarray(HEAD_DIM ** (-0.5), bf16)
        return carry

    lax.fori_loop(0, slots // 2, queries_step, 0)
    keys_ready()
    for entry in range(slots * per_slot + GROUP):
        table[entry] = 0
    total = 0
    for slot in range(slots):
        for block in range(per_slot):
            table[total + block] = slot * per_slot + block
        total = total + blocks_of(lengths[slots * tile + slot])

    def keys_step(group, carry):
        tokens = []
        for i in range(GROUP):
            entry = table[group * GROUP + i]
            row = pl.multiple_of(entry % per_slot * KEY_BLOCK, KEY_BLOCK)
            tokens.append(x[slots * tile + entry // per_slot, pl.ds(row, KEY_BLOCK), :])
        tokens = jnp.concatenate(tokens, axis=0)
        for kept, start in ((keys, D), (values, 2 * D)):
            lanes = slice(start, start + D)
            found = (product(tokens, qkv_w[:, lanes]) + qkv_bias[:, lanes]).astype(bf16)
            for i in range(GROUP):
                row = pl.multiple_of(table[group * GROUP + i] * KEY_BLOCK, KEY_BLOCK)
                kept[pl.ds(row, KEY_BLOCK), :] = found[i * KEY_BLOCK : (i + 1) * KEY_BLOCK]
        return carry

    lax.fori_loop(0, (total + GROUP - 1) // GROUP, keys_step, 0)


def two_heads(low, block):
    zero = jnp.zeros((), block.dtype)
    return jnp.concatenate([jnp.where(low, block, zero), jnp.where(low, zero, block)], axis=0)


def visible_rows(start, length):
    return start + lax.broadcasted_iota(jnp.int32, (KEY_BLOCK, LANES), 0) < length


def attend(slot, blocks, length, queries, keys, values, contexts, extremes):
    low = lax.broadcasted_iota(jnp.int32, (1, LANES), 1) < HEAD_DIM
    half = contexts[0].shape[0]
    seen = blocks * KEY_BLOCK
    base = slot * 2 * half
    visible = visible_rows(seen - KEY_BLOCK, length)
    ones = two_heads(low, jnp.ones((KEY_BLOCK, LANES), bf16))
    ones_last = two_heads(low, jnp.where(visible, 1.0, 0.0).astype(bf16))
    extreme = None
    for pair in range(0, D, LANES):
        lanes = slice(pair, pair + LANES)
        key_blocks, value_blocks = [], []
        for start in range(0, seen, KEY_BLOCK):
            rows = pl.ds(pl.multiple_of(base + start, KEY_BLOCK), KEY_BLOCK)
            value_block, counted = values[rows, lanes], ones
            if start + KEY_BLOCK == seen:
                value_block = jnp.where(visible, value_block, jnp.zeros((), bf16))
                counted = ones_last
            key_blocks.append(two_heads(low, keys[rows, lanes]))
            value_blocks.append(jnp.concatenate([two_heads(low, value_block), counted], axis=1))
        for part, context in enumerate(contexts):
            rows = pl.ds(pl.multiple_of(base + part * half, half), half)
            mine = queries[rows, lanes]
            total = None
            for key_block, value_block in zip(key_blocks, value_blocks):
                scores = lax.dot_general(mine, key_block, ROWS_BY_ROWS, preferred_element_type=f32)
                term = product(jnp.exp(scores).astype(bf16), value_block)
                total = term if total is None else total + term
            sums = total[:, LANES:]
            inverse = 1.0 / sums
            context[:, lanes] = (total[:, :LANES] * inverse).astype(bf16)
            farthest = jnp.max(jnp.maximum(sums, inverse).reshape(half // 8, 8, LANES), axis=0)
            extreme = farthest if extreme is None else jnp.maximum(extreme, farthest)
    extremes[...] = extreme


def attend_shifted(slot, length, queries, keys, values, contexts):
    low = lax.broadcasted_iota(jnp.int32, (1, LANES), 1) < HEAD_DIM
    half = contexts[0].shape[0]
    base = slot * 2 * half

    def pair_step(pair, carry):
        lanes = pl.ds(pl.multiple_of(pair * LANES, LANES), LANES)
        key_blocks, value_blocks = [], []
        for start in range(0, 2 * half, KEY_BLOCK):
            rows = pl.ds(pl.multiple_of(base + start, KEY_BLOCK), KEY_BLOCK)
            visible = visible_rows(start, length)
            key_block, value_block = keys[rows, lanes], values[rows, lanes]
            if start == 0:
                first_key = key_block[0:1, :]
            key_blocks.append(two_heads(low, jnp.where(visible, key_block, first_key)))
            value_block = jnp.where(visible, value_block, jnp.zeros((), bf16))
            counted = jnp.where(visible, 1.0, 0.0).astype(bf16)
            value_blocks.append(jnp.concatenate([two_heads(low, value_block), two_heads(low, counted)], axis=1))

        def rows_step(context, start, step):
            offset = pl.multiple_of(step * KEY_BLOCK, KEY_BLOCK)
            mine = queries[pl.ds(pl.multiple_of(base + start + offset, KEY_BLOCK), KEY_BLOCK), lanes]
            scores = [lax.dot_general(mine, block, ROWS_BY_ROWS, preferred_element_type=f32) for block in key_blocks]
            top = functools.reduce(jnp.maximum, scores)
            top_low = jnp.max(top[:, :KEY_BLOCK], axis=-1, keepdims=True)
            top_high = jnp.max(top[:, KEY_BLOCK:], axis=-1, keepdims=True)
            total = None
            for score, block in zip(scores, value_blocks):
                shifted = jnp.concatenate([score[:, :KEY_BLOCK] - top_low, score[:, KEY_BLOCK:] - top_high], axis=1)
                term = product(jnp.exp(shifted).astype(bf16), block)
                total = term if total is None else total + term
            context[pl.ds(offset, KEY_BLOCK), lanes] = (total[:, :LANES] / total[:, LANES:]).astype(bf16)

        for part, context in enumerate(contexts):

            def step(i, carry, part=part, context=context):
                rows_step(context, part * half, i)
                return carry

            lax.fori_loop(0, half // KEY_BLOCK, step, 0)
        return carry

    lax.fori_loop(0, D // LANES, pair_step, 0)


def close_attention(slot, first, x, context, out_w, vectors, after):
    out_bias, attention_gain, attention_shift = vectors
    slots, half = after.shape[0], after.shape[1]
    for j in range(slots):
        attended = product(context[j], out_w[...]) + out_bias
        tokens = x[slot + j, first : first + half, :].astype(f32)
        after[j] = layer_norm(tokens + attended, attention_gain, attention_shift)


def feed_forward(tile, up_w, down_w, vectors, active, after, result, emit=None):
    up_bias, down_bias, output_gain, output_shift = vectors
    per_tile, half = after.shape[0], after.shape[1]
    total = per_tile * half
    for chunk in range(FF // D):
        spot = slice(chunk * D, (chunk + 1) * D)
        for j in range(0, per_tile, 2):
            rows = after[j : j + 2].reshape(2 * half, D).astype(bf16)
            expanded = product(rows, up_w[:, spot]) + up_bias[:, spot]
            active[chunk * total + j * half : chunk * total + (j + 2) * half, :] = gelu(expanded).astype(bf16)
    for j in range(per_tile):
        spread = [active[chunk * total + j * half : chunk * total + (j + 1) * half, :] for chunk in range(FF // D)]
        second = product(jnp.concatenate(spread, axis=1), down_w[...]) + down_bias
        done = layer_norm(after[j] + second, output_gain, output_shift).astype(bf16)
        result[per_tile * tile + j] = done
        if emit is not None:
            emit(per_tile * tile + j, done)


def vectors_of(held):
    widths = (3 * D, D, D, D, FF, D, D, D)
    return [held[i : i + 1, :width] for i, width in enumerate(widths)]


def first_kernel(lengths, labels, x_hbm, qkv_hbm, out_hbm, up_hbm, down_hbm, *rest):
    vectors_hbm = rest[:8]
    hidden_hbm, later_hbm, leads_hbm, out_w, held = rest[8:13]
    x, later, up_w, down_w, qkv_w, lead, context, table, queries, keys, values, extremes, after, active, result, load_sem, x_sem, store_sem, vector_sem, later_sem, lead_sem = rest[13:]
    slots = x.shape[0]
    half = result.shape[1]
    per_tile = result.shape[0] // TILES

    def load_x(slot):
        return pltpu.make_async_copy(x_hbm.at[slot], x.at[slot], x_sem.at[slot])

    sources = [(qkv_hbm.at[:, spot], qkv_w.at[:, spot]) for spot in (pl.ds(0, D), pl.ds(D, 2 * D))]
    sources += [(out_hbm, out_w), (up_hbm, up_w), (down_hbm, down_w)]
    loads = [pltpu.make_async_copy(a, b, load_sem.at[i]) for i, (a, b) in enumerate(sources)]
    small = [
        pltpu.make_async_copy(ref, held.at[i, pl.ds(0, ref.shape[0])], vector_sem.at[i])
        for i, ref in enumerate(vectors_hbm)
    ]
    for copy in (loads[0], load_x(0), load_x(1), *small):
        copy.start()

    def store(slot):
        return pltpu.make_async_copy(result.at[slot], hidden_hbm.at[slot, pl.ds(0, half), :], store_sem.at[slot])

    def store_later(slot):
        return pltpu.make_async_copy(later.at[slot], later_hbm.at[slot], later_sem.at[slot])

    for copy in (loads[0], *small):
        copy.wait()
    loads[1].start()
    for slot in range(2, slots):
        load_x(slot).start()
    vectors = vectors_of(held)

    def contexts_of(tile, j):
        return context.at[j], later.at[per_tile * tile + j]

    def attention_step(tile):
        def step(j, carry):
            length = lengths[per_tile * tile + j]
            for blocks in range(1, x.shape[1] // KEY_BLOCK + 1):

                @pl.when(blocks_of(length) == blocks)
                def _():
                    attend(j, blocks, length, queries, keys, values, contexts_of(tile, j), extremes.at[j])

            return carry

        return step

    def shifted_step(tile):
        def step(j, carry):
            length = lengths[per_tile * tile + j]
            attend_shifted(j, length, queries, keys, values, contexts_of(tile, j))
            return carry

        return step

    def emit(slot, done):
        store(slot).start()
        place = lax.broadcasted_iota(jnp.int32, (1, EXTRA), 1)
        facts = jnp.where(place == 0, lengths[slot], labels[slot]).astype(f32)
        lead[pl.ds(slot, 1), :] = jnp.concatenate([done[0:1, :].astype(f32), facts], axis=1)

    def tile_step(tile, carry):
        def keys_ready():
            @pl.when(tile == 0)
            def _():
                loads[1].wait()
                for load in loads[2:]:
                    load.start()

        project(tile, x, load_x, lengths, qkv_w, vectors[0], table, queries, keys, values, keys_ready)
        lax.fori_loop(0, per_tile, attention_step(tile), 0)

        @pl.when(jnp.logical_not(jnp.max(extremes[...]) <= SAFE))
        def _():
            lax.fori_loop(0, per_tile, shifted_step(tile), 0)

        for j in range(per_tile):
            store_later(per_tile * tile + j).start()

        @pl.when(tile == 0)
        def _():
            for load in loads[2:]:
                load.wait()

        close_attention(per_tile * tile, 0, x, context, out_w, vectors[1:4], after)
        feed_forward(tile, up_w, down_w, vectors[4:], active, after, result, emit)
        return carry

    lax.fori_loop(0, TILES, tile_step, 0)
    def each_device(act):
        def step(device, carry):
            act(pltpu.make_async_copy(lead, leads_hbm.at[device], lead_sem.at[device]))
            return carry

        lax.fori_loop(0, leads_hbm.shape[0], step, 0)

    each_device(lambda copy: copy.start())
    each_device(lambda copy: copy.wait())
    for slot in range(slots):
        store(slot).wait()
        store_later(slot).wait()


def second_kernel(
    x_hbm, context_hbm, up_hbm, down_hbm, out_w, held, hidden_in_place, hidden_hbm,
    x, context, up_w, down_w, after, active, result, load_sem, x_sem, context_sem, store_sem,
):
    slots, half = result.shape[:2]
    per_tile = slots // TILES
    vectors = vectors_of(held)

    def load_rows(step):
        spot = pl.ds(2 * step, 2)
        return (
            pltpu.make_async_copy(context_hbm.at[spot], context.at[spot], context_sem.at[step]),
            pltpu.make_async_copy(x_hbm.at[spot, pl.ds(half, half), :], x.at[spot], x_sem.at[step]),
        )

    sources = [(up_hbm, up_w), (down_hbm, down_w)]
    loads = [pltpu.make_async_copy(a, b, load_sem.at[i]) for i, (a, b) in enumerate(sources)]
    for copy in load_rows(0):
        copy.start()
    for step in range(1, slots // 2):
        for copy in load_rows(step):
            copy.start()
    for load in loads:
        load.start()

    def store(slot):
        return pltpu.make_async_copy(
            result.at[slot], hidden_hbm.at[slot, pl.ds(half, half), :], store_sem.at[slot]
        )

    def attention_step(step, carry):
        for copy in load_rows(step):
            copy.wait()
        mine = pl.ds(2 * step, 2)
        close_attention(2 * step, 0, x, context.at[mine], out_w, vectors[1:4], after.at[mine])
        return carry

    def tile_step(tile, carry):
        mine = pl.ds(per_tile * tile, per_tile)
        feed_forward(tile, up_w, down_w, vectors[4:], active, after.at[mine], result, lambda slot, _: store(slot).start())
        return carry

    lax.fori_loop(0, slots // 2, attention_step, 0)
    for load in loads:
        load.wait()
    lax.fori_loop(0, TILES, tile_step, 0)
    for slot in range(slots):
        store(slot).wait()


def ramp_kernel(gathered, pooler_w, pooler_b, ramp_t, ramp_b, logits_out, gpw_out, gpb_out, grw_out, grb_out, entropy_out, scored, found, sem):
    own = logits_out.shape[1]
    leading = gathered[:, :D].astype(bf16)
    lengths = gathered[:, D : D + 1]
    labels = gathered[:, D + 1 : D + 2]
    pooled = jnp.tanh(product(leading, pooler_w[...]) + pooler_b[...].reshape(1, -1))
    ramp = [ramp_t[c : c + 1, :] for c in range(CLASSES)]
    bias = ramp_b[...].reshape(1, -1)
    logits = [jnp.sum(pooled * ramp[c], axis=1, keepdims=True) + bias[:, c : c + 1] for c in range(CLASSES)]
    scored[...] = jnp.concatenate(logits, axis=1)
    wide, narrow = lax.axis_index(AXES[0]), lax.axis_index(AXES[1])
    place = wide * lax.axis_size(AXES[1]) + narrow
    logits_out[...] = scored[pl.ds(pl.multiple_of(place * own, own), own), :].T
    top = functools.reduce(jnp.maximum, logits)
    shifted = [one - top for one in logits]
    powers = [jnp.exp(one) for one in shifted]
    total = sum(powers[1:], powers[0])
    dlogits = [powers[c] / total - jnp.where(labels == float(c), 1.0, 0.0) for c in range(CLASSES)]
    back = sum((dlogits[c] * ramp[c] for c in range(1, CLASSES)), dlogits[0] * ramp[0])
    pooled_grad = (back * (1.0 - pooled * pooled)).astype(bf16)
    copies = []
    for i in range(D // QUAD):
        rows = slice(i * QUAD, (i + 1) * QUAD)
        found[rows, :] = lax.dot_general(leading[:, rows], pooled_grad, COLS_BY_COLS, preferred_element_type=f32)
        copies.append(pltpu.make_async_copy(found.at[rows], gpw_out.at[rows], sem.at[i]))
        copies[i].start()
    gpb_out[...] = jnp.sum(pooled_grad.astype(f32), axis=0)
    for c in range(CLASSES):
        grw_out[c : c + 1, :] = jnp.sum(pooled * dlogits[c], axis=0, keepdims=True)
    grb_out[...] = jnp.concatenate([jnp.sum(one, axis=0) for one in dlogits])
    log_total = jnp.log(total)
    log_probs = [one - log_total for one in shifted]
    row_entropy = -sum((jnp.exp(one) * one for one in log_probs[1:]), jnp.exp(log_probs[0]) * log_probs[0])
    entropy_out[...] = jnp.sum(lengths * row_entropy, axis=0, keepdims=True) / jnp.sum(lengths, axis=0, keepdims=True)
    for copy in copies:
        copy.wait()


VMEM_LIMIT = 56 * 1024 * 1024
SECOND_LIMIT = 42 * 1024 * 1024


def local(
    hidden_in, lengths, labels,
    qkv_weight, qkv_bias, out_weight, out_bias, attention_gain, attention_shift,
    up_weight, up_bias, down_weight, down_bias, output_gain, output_shift,
    pooler_weight, pooler_bias, ramp_weight, ramp_bias,
):
    slots = lengths.shape[0]
    length = hidden_in.shape[0] // slots
    half = length // 2
    rows = slots // TILES * half
    shape = (slots, length, D)
    devices = lax.axis_size(AXES)
    sequences = hidden_in.reshape(shape)
    vectors = (qkv_bias, out_bias, attention_gain, attention_shift, up_bias, down_bias, output_gain, output_shift)
    anywhere = pl.BlockSpec(memory_space=pltpu.HBM)
    in_hbm = lambda array: pltpu.with_memory_space_constraint(array, pltpu.HBM)
    scalars = pl.BlockSpec(memory_space=pltpu.SMEM)
    vmem = pl.BlockSpec(memory_space=pltpu.VMEM)
    dma = pltpu.SemaphoreType.DMA
    weights = [pltpu.VMEM(one, bf16) for one in ((D, FF), (FF, D))]
    common = [
        pltpu.VMEM((rows * FF // D, D), bf16),
        pltpu.VMEM((slots, half, D), bf16),
    ]
    cost = pl.CostEstimate(
        flops=2 * slots * half * D * (2 * D + 2 * FF + 2 * length), bytes_accessed=30_000_000, transcendentals=0
    )
    params = pltpu.CompilerParams(vmem_limit_bytes=VMEM_LIMIT)
    hidden, later, leads, *kept = pl.pallas_call(
        first_kernel,
        name="first_half",
        out_shape=[
            pltpu.HBM(shape, bf16),
            pltpu.HBM((slots, half, D), bf16),
            pltpu.HBM((devices, slots, D + EXTRA), f32),
            pltpu.VMEM((D, D), bf16),
            pltpu.VMEM((len(vectors), FF), f32),
        ],
        in_specs=[scalars] * 2 + [anywhere] * 13,
        out_specs=[anywhere] * 3 + [vmem] * 2,
        scratch_shapes=[pltpu.VMEM(shape, bf16), pltpu.VMEM((slots, half, D), bf16)]
        + weights
        + [
            pltpu.VMEM((D, 3 * D), bf16),
            pltpu.VMEM((slots, D + EXTRA), f32),
            pltpu.VMEM((slots // TILES, half, D), bf16),
            pltpu.SMEM((slots // TILES * length // KEY_BLOCK + GROUP,), jnp.int32),
            pltpu.VMEM((2 * rows, D), bf16),
            pltpu.VMEM((2 * rows, D), bf16),
            pltpu.VMEM((2 * rows, D), bf16),
            pltpu.VMEM((slots // TILES, 8, LANES), f32),
        ]
        + [pltpu.VMEM((slots // TILES, half, D), f32)]
        + common
        + [dma((5,)), dma((slots,)), dma((slots,)), dma((len(vectors),)), dma((slots,)), dma((devices,))],
        compiler_params=params,
        cost_estimate=cost,
    )(lengths, labels, *[in_hbm(a) for a in (sequences, qkv_weight, out_weight, up_weight, down_weight, *vectors)])
    gathered = lax.all_to_all(leads, AXES, 0, 0).reshape(devices * slots, D + EXTRA)
    hidden = pl.pallas_call(
        second_kernel,
        name="second_half",
        out_shape=pltpu.HBM(shape, bf16),
        in_specs=[anywhere] * 4 + [vmem] * 2 + [anywhere],
        out_specs=anywhere,
        scratch_shapes=[pltpu.VMEM((slots, half, D), bf16)] * 2
        + weights
        + [pltpu.VMEM((slots, half, D), f32)]
        + common
        + [dma((2,)), dma((slots // 2,)), dma((slots // 2,)), dma((slots,))],
        input_output_aliases={6: 0},
        compiler_params=pltpu.CompilerParams(vmem_limit_bytes=SECOND_LIMIT),
        cost_estimate=cost,
    )(
        *[in_hbm(a) for a in (sequences, later, up_weight, down_weight)],
        *[pltpu.with_memory_space_constraint(a, pltpu.VMEM) for a in kept],
        in_hbm(hidden),
    )
    one = lambda *shape: jax.ShapeDtypeStruct(shape, f32)
    logits, gpw, gpb, grw, grb, entropy = pl.pallas_call(
        ramp_kernel,
        name="off_ramp",
        out_shape=[one(CLASSES, slots), pltpu.HBM((D, D), f32), one(D), one(CLASSES, D), one(CLASSES), one(1, 1)],
        in_specs=[vmem] * 5,
        out_specs=[vmem, anywhere] + [vmem] * 4,
        scratch_shapes=[pltpu.VMEM((devices * slots, CLASSES), f32), pltpu.VMEM((D, D), f32), dma((D // QUAD,))],
        compiler_params=pltpu.CompilerParams(vmem_limit_bytes=8 * 1024 * 1024 + 5 * 4 * gathered.size),
    )(gathered, pooler_weight, pooler_bias, ramp_weight.T, ramp_bias)
    return hidden.reshape(hidden_in.shape), logits.T, gpw, gpb, grw.T, grb, entropy.reshape(())


def solution(mesh):
    spread = P(AXES)
    placed = (P(AXES, None), spread, spread) + (P(),) * 16
    return jax.shard_map(
        local,
        mesh=mesh,
        in_specs=placed,
        out_specs=(P(AXES, None), P(AXES, None), P(), P(), P(), P(), P()),
        check_vma=False,
    )
```

```python
import functools

import jax
import jax.numpy as jnp
from jax import lax
from jax.experimental import pallas as pl
from jax.experimental.pallas import tpu as pltpu
from jax.sharding import PartitionSpec as P

D = 768
HEADS = 12
HEAD_DIM = 64
FF = 3072
CLASSES = 3
LANES = 128
KEY_BLOCK = 128
QUAD = 2 * LANES
GROUP = 4
EXTRA = 128
SAFE = 1e25
TILES = 2

AXES = ("wide", "narrow")
ROWS_BY_ROWS = (((1,), (1,)), ((), ()))
COLS_BY_COLS = (((0,), (0,)), ((), ()))
f32 = jnp.float32
bf16 = jnp.bfloat16


def product(left, right):
    return jnp.dot(left, right, preferred_element_type=f32)


def layer_norm(values, gain, shift):
    center = values - jnp.mean(values, axis=-1, keepdims=True)
    spread = jnp.mean(center * center, axis=-1, keepdims=True)
    return center * lax.rsqrt(spread + 1e-12) * gain + shift


def gelu(values):
    half = 0.5 * values
    return half + half * lax.erf(values * 0.7071067811865476)


def blocks_of(length):
    return (length + KEY_BLOCK - 1) // KEY_BLOCK


def project(tile, x, load_x, lengths, qkv_w, qkv_bias, table, queries, keys, values, keys_ready):
    slots, length = x.shape[0] // TILES, x.shape[1]
    per_slot = length // KEY_BLOCK

    def queries_step(step, carry):
        first = slots * tile + 2 * step
        for i in range(2):
            load_x(first + i).wait()
        tokens = x[pl.ds(first, 2)].reshape(2 * length, D)
        rows = pl.ds(pl.multiple_of(2 * length * step, 2 * length), 2 * length)
        for start in range(0, D, QUAD):
            lanes = slice(start, start + QUAD)
            found = (product(tokens, qkv_w[:, lanes]) + qkv_bias[:, lanes]).astype(bf16)
            queries[rows, lanes] = found * jnp.asarray(HEAD_DIM ** (-0.5), bf16)
        return carry

    lax.fori_loop(0, slots // 2, queries_step, 0)
    keys_ready()
    for entry in range(slots * per_slot + GROUP):
        table[entry] = 0
    total = 0
    for slot in range(slots):
        for block in range(per_slot):
            table[total + block] = slot * per_slot + block
        total = total + blocks_of(lengths[slots * tile + slot])

    def keys_step(group, carry):
        tokens = []
        for i in range(GROUP):
            entry = table[group * GROUP + i]
            row = pl.multiple_of(entry % per_slot * KEY_BLOCK, KEY_BLOCK)
            tokens.append(x[slots * tile + entry // per_slot, pl.ds(row, KEY_BLOCK), :])
        tokens = jnp.concatenate(tokens, axis=0)
        for kept, start in ((keys, D), (values, 2 * D)):
            lanes = slice(start, start + D)
            found = (product(tokens, qkv_w[:, lanes]) + qkv_bias[:, lanes]).astype(bf16)
            for i in range(GROUP):
                row = pl.multiple_of(table[group * GROUP + i] * KEY_BLOCK, KEY_BLOCK)
                kept[pl.ds(row, KEY_BLOCK), :] = found[i * KEY_BLOCK : (i + 1) * KEY_BLOCK]
        return carry

    lax.fori_loop(0, (total + GROUP - 1) // GROUP, keys_step, 0)


def two_heads(low, block):
    zero = jnp.zeros((), block.dtype)
    return jnp.concatenate([jnp.where(low, block, zero), jnp.where(low, zero, block)], axis=0)


def visible_rows(start, length):
    return start + lax.broadcasted_iota(jnp.int32, (KEY_BLOCK, LANES), 0) < length


def attend(slot, blocks, length, queries, keys, values, contexts, extremes):
    low = lax.broadcasted_iota(jnp.int32, (1, LANES), 1) < HEAD_DIM
    half = contexts[0].shape[0]
    seen = blocks * KEY_BLOCK
    base = slot * 2 * half
    visible = visible_rows(seen - KEY_BLOCK, length)
    ones = two_heads(low, jnp.ones((KEY_BLOCK, LANES), bf16))
    ones_last = two_heads(low, jnp.where(visible, 1.0, 0.0).astype(bf16))
    extreme = None
    for pair in range(0, D, LANES):
        lanes = slice(pair, pair + LANES)
        key_blocks, value_blocks = [], []
        for start in range(0, seen, KEY_BLOCK):
            rows = pl.ds(pl.multiple_of(base + start, KEY_BLOCK), KEY_BLOCK)
            value_block, counted = values[rows, lanes], ones
            if start + KEY_BLOCK == seen:
                value_block = jnp.where(visible, value_block, jnp.zeros((), bf16))
                counted = ones_last
            key_blocks.append(two_heads(low, keys[rows, lanes]))
            value_blocks.append(jnp.concatenate([two_heads(low, value_block), counted], axis=1))
        for part, context in enumerate(contexts):
            rows = pl.ds(pl.multiple_of(base + part * half, half), half)
            mine = queries[rows, lanes]
            wide = [
                jnp.exp(lax.dot_general(mine, block, ROWS_BY_ROWS, preferred_element_type=f32)).astype(bf16)
                for block in key_blocks
            ]
            total = product(jnp.concatenate(wide, axis=1), jnp.concatenate(value_blocks, axis=0))
            sums = total[:, LANES:]
            inverse = 1.0 / sums
            context[:, lanes] = (total[:, :LANES] * inverse).astype(bf16)
            farthest = jnp.max(jnp.maximum(sums, inverse).reshape(half // 8, 8, LANES), axis=0)
            extreme = farthest if extreme is None else jnp.maximum(extreme, farthest)
    extremes[...] = extreme


def attend_shifted(slot, length, queries, keys, values, contexts):
    low = lax.broadcasted_iota(jnp.int32, (1, LANES), 1) < HEAD_DIM
    half = contexts[0].shape[0]
    base = slot * 2 * half

    def pair_step(pair, carry):
        lanes = pl.ds(pl.multiple_of(pair * LANES, LANES), LANES)
        key_blocks, value_blocks = [], []
        for start in range(0, 2 * half, KEY_BLOCK):
            rows = pl.ds(pl.multiple_of(base + start, KEY_BLOCK), KEY_BLOCK)
            visible = visible_rows(start, length)
            key_block, value_block = keys[rows, lanes], values[rows, lanes]
            if start == 0:
                first_key = key_block[0:1, :]
            key_blocks.append(two_heads(low, jnp.where(visible, key_block, first_key)))
            value_block = jnp.where(visible, value_block, jnp.zeros((), bf16))
            counted = jnp.where(visible, 1.0, 0.0).astype(bf16)
            value_blocks.append(jnp.concatenate([two_heads(low, value_block), two_heads(low, counted)], axis=1))

        def rows_step(context, start, step):
            offset = pl.multiple_of(step * KEY_BLOCK, KEY_BLOCK)
            mine = queries[pl.ds(pl.multiple_of(base + start + offset, KEY_BLOCK), KEY_BLOCK), lanes]
            scores = [lax.dot_general(mine, block, ROWS_BY_ROWS, preferred_element_type=f32) for block in key_blocks]
            top = functools.reduce(jnp.maximum, scores)
            top_low = jnp.max(top[:, :KEY_BLOCK], axis=-1, keepdims=True)
            top_high = jnp.max(top[:, KEY_BLOCK:], axis=-1, keepdims=True)
            total = None
            for score, block in zip(scores, value_blocks):
                shifted = jnp.concatenate([score[:, :KEY_BLOCK] - top_low, score[:, KEY_BLOCK:] - top_high], axis=1)
                term = product(jnp.exp(shifted).astype(bf16), block)
                total = term if total is None else total + term
            context[pl.ds(offset, KEY_BLOCK), lanes] = (total[:, :LANES] / total[:, LANES:]).astype(bf16)

        for part, context in enumerate(contexts):

            def step(i, carry, part=part, context=context):
                rows_step(context, part * half, i)
                return carry

            lax.fori_loop(0, half // KEY_BLOCK, step, 0)
        return carry

    lax.fori_loop(0, D // LANES, pair_step, 0)


def close_attention(slot, first, x, context, out_w, vectors, after):
    out_bias, attention_gain, attention_shift = vectors
    slots, half = after.shape[0], after.shape[1]
    for j in range(slots):
        attended = product(context[j], out_w[...]) + out_bias
        tokens = x[slot + j, first : first + half, :].astype(f32)
        after[j] = layer_norm(tokens + attended, attention_gain, attention_shift)


def feed_forward(tile, up_w, down_w, vectors, active, after, result, emit=None):
    up_bias, down_bias, output_gain, output_shift = vectors
    per_tile, half = after.shape[0], after.shape[1]
    total = per_tile * half
    for chunk in range(FF // D):
        spot = slice(chunk * D, (chunk + 1) * D)
        for j in range(0, per_tile, 2):
            rows = after[j : j + 2].reshape(2 * half, D).astype(bf16)
            expanded = product(rows, up_w[:, spot]) + up_bias[:, spot]
            active[chunk * total + j * half : chunk * total + (j + 2) * half, :] = gelu(expanded).astype(bf16)
    for j in range(per_tile):
        spread = [active[chunk * total + j * half : chunk * total + (j + 1) * half, :] for chunk in range(FF // D)]
        second = product(jnp.concatenate(spread, axis=1), down_w[...]) + down_bias
        done = layer_norm(after[j] + second, output_gain, output_shift).astype(bf16)
        result[per_tile * tile + j] = done
        if emit is not None:
            emit(per_tile * tile + j, done)


def vectors_of(held):
    widths = (3 * D, D, D, D, FF, D, D, D)
    return [held[i : i + 1, :width] for i, width in enumerate(widths)]


def first_kernel(lengths, labels, x_hbm, qkv_hbm, out_hbm, up_hbm, down_hbm, *rest):
    vectors_hbm = rest[:8]
    hidden_hbm, later_hbm, leads_hbm, out_w, held = rest[8:13]
    x, later, up_w, down_w, qkv_w, lead, context, table, queries, keys, values, extremes, after, active, result, load_sem, x_sem, store_sem, vector_sem, later_sem, lead_sem = rest[13:]
    slots = x.shape[0]
    half = result.shape[1]
    per_tile = result.shape[0] // TILES

    def load_x(slot):
        return pltpu.make_async_copy(x_hbm.at[slot], x.at[slot], x_sem.at[slot])

    sources = [(qkv_hbm.at[:, spot], qkv_w.at[:, spot]) for spot in (pl.ds(0, D), pl.ds(D, 2 * D))]
    sources += [(out_hbm, out_w), (up_hbm, up_w), (down_hbm, down_w)]
    loads = [pltpu.make_async_copy(a, b, load_sem.at[i]) for i, (a, b) in enumerate(sources)]
    small = [
        pltpu.make_async_copy(ref, held.at[i, pl.ds(0, ref.shape[0])], vector_sem.at[i])
        for i, ref in enumerate(vectors_hbm)
    ]
    for copy in (loads[0], load_x(0), load_x(1), *small):
        copy.start()

    def store(slot):
        return pltpu.make_async_copy(result.at[slot], hidden_hbm.at[slot, pl.ds(0, half), :], store_sem.at[slot])

    def store_later(slot):
        return pltpu.make_async_copy(later.at[slot], later_hbm.at[slot], later_sem.at[slot])

    for copy in (loads[0], *small):
        copy.wait()
    loads[1].start()
    for slot in range(2, slots):
        load_x(slot).start()
    vectors = vectors_of(held)

    def contexts_of(tile, j):
        return context.at[j], later.at[per_tile * tile + j]

    def attention_step(tile):
        def step(j, carry):
            length = lengths[per_tile * tile + j]
            for blocks in range(1, x.shape[1] // KEY_BLOCK + 1):

                @pl.when(blocks_of(length) == blocks)
                def _():
                    attend(j, blocks, length, queries, keys, values, contexts_of(tile, j), extremes.at[j])

            return carry

        return step

    def shifted_step(tile):
        def step(j, carry):
            length = lengths[per_tile * tile + j]
            attend_shifted(j, length, queries, keys, values, contexts_of(tile, j))
            return carry

        return step

    def emit(slot, done):
        store(slot).start()
        place = lax.broadcasted_iota(jnp.int32, (1, EXTRA), 1)
        facts = jnp.where(place == 0, lengths[slot], labels[slot]).astype(f32)
        lead[pl.ds(slot, 1), :] = jnp.concatenate([done[0:1, :].astype(f32), facts], axis=1)

    def tile_step(tile, carry):
        def keys_ready():
            @pl.when(tile == 0)
            def _():
                loads[1].wait()
                for load in loads[2:]:
                    load.start()

        project(tile, x, load_x, lengths, qkv_w, vectors[0], table, queries, keys, values, keys_ready)
        lax.fori_loop(0, per_tile, attention_step(tile), 0)

        @pl.when(jnp.logical_not(jnp.max(extremes[...]) <= SAFE))
        def _():
            lax.fori_loop(0, per_tile, shifted_step(tile), 0)

        for j in range(per_tile):
            store_later(per_tile * tile + j).start()

        @pl.when(tile == 0)
        def _():
            for load in loads[2:]:
                load.wait()

        close_attention(per_tile * tile, 0, x, context, out_w, vectors[1:4], after)
        feed_forward(tile, up_w, down_w, vectors[4:], active, after, result, emit)
        return carry

    lax.fori_loop(0, TILES, tile_step, 0)
    def each_device(act):
        def step(device, carry):
            act(pltpu.make_async_copy(lead, leads_hbm.at[device], lead_sem.at[device]))
            return carry

        lax.fori_loop(0, leads_hbm.shape[0], step, 0)

    each_device(lambda copy: copy.start())
    each_device(lambda copy: copy.wait())
    for slot in range(slots):
        store(slot).wait()
        store_later(slot).wait()


def second_kernel(
    x_hbm, context_hbm, up_hbm, down_hbm, out_w, held, hidden_in_place, hidden_hbm,
    x, context, up_w, down_w, after, active, result, load_sem, x_sem, context_sem, store_sem,
):
    slots, half = result.shape[:2]
    per_tile = slots // TILES
    vectors = vectors_of(held)

    def load_rows(step):
        spot = pl.ds(2 * step, 2)
        return (
            pltpu.make_async_copy(context_hbm.at[spot], context.at[spot], context_sem.at[step]),
            pltpu.make_async_copy(x_hbm.at[spot, pl.ds(half, half), :], x.at[spot], x_sem.at[step]),
        )

    sources = [(up_hbm, up_w), (down_hbm, down_w)]
    loads = [pltpu.make_async_copy(a, b, load_sem.at[i]) for i, (a, b) in enumerate(sources)]
    for copy in load_rows(0):
        copy.start()
    for step in range(1, slots // 2):
        for copy in load_rows(step):
            copy.start()
    for load in loads:
        load.start()

    def store(slot):
        return pltpu.make_async_copy(
            result.at[slot], hidden_hbm.at[slot, pl.ds(half, half), :], store_sem.at[slot]
        )

    def attention_step(step, carry):
        for copy in load_rows(step):
            copy.wait()
        mine = pl.ds(2 * step, 2)
        close_attention(2 * step, 0, x, context.at[mine], out_w, vectors[1:4], after.at[mine])
        return carry

    def tile_step(tile, carry):
        mine = pl.ds(per_tile * tile, per_tile)
        feed_forward(tile, up_w, down_w, vectors[4:], active, after.at[mine], result, lambda slot, _: store(slot).start())
        return carry

    lax.fori_loop(0, slots // 2, attention_step, 0)
    for load in loads:
        load.wait()
    lax.fori_loop(0, TILES, tile_step, 0)
    for slot in range(slots):
        store(slot).wait()


def ramp_kernel(gathered, pooler_w, pooler_b, ramp_t, ramp_b, logits_out, gpw_out, gpb_out, grw_out, grb_out, entropy_out, scored, found, sem):
    own = logits_out.shape[1]
    leading = gathered[:, :D].astype(bf16)
    lengths = gathered[:, D : D + 1]
    labels = gathered[:, D + 1 : D + 2]
    pooled = jnp.tanh(product(leading, pooler_w[...]) + pooler_b[...].reshape(1, -1))
    ramp = [ramp_t[c : c + 1, :] for c in range(CLASSES)]
    bias = ramp_b[...].reshape(1, -1)
    logits = [jnp.sum(pooled * ramp[c], axis=1, keepdims=True) + bias[:, c : c + 1] for c in range(CLASSES)]
    scored[...] = jnp.concatenate(logits, axis=1)
    wide, narrow = lax.axis_index(AXES[0]), lax.axis_index(AXES[1])
    place = wide * lax.axis_size(AXES[1]) + narrow
    logits_out[...] = scored[pl.ds(pl.multiple_of(place * own, own), own), :].T
    top = functools.reduce(jnp.maximum, logits)
    shifted = [one - top for one in logits]
    powers = [jnp.exp(one) for one in shifted]
    total = sum(powers[1:], powers[0])
    dlogits = [powers[c] / total - jnp.where(labels == float(c), 1.0, 0.0) for c in range(CLASSES)]
    back = sum((dlogits[c] * ramp[c] for c in range(1, CLASSES)), dlogits[0] * ramp[0])
    pooled_grad = (back * (1.0 - pooled * pooled)).astype(bf16)
    copies = []
    for i in range(D // QUAD):
        rows = slice(i * QUAD, (i + 1) * QUAD)
        found[rows, :] = lax.dot_general(leading[:, rows], pooled_grad, COLS_BY_COLS, preferred_element_type=f32)
        copies.append(pltpu.make_async_copy(found.at[rows], gpw_out.at[rows], sem.at[i]))
        copies[i].start()
    gpb_out[...] = jnp.sum(pooled_grad.astype(f32), axis=0)
    for c in range(CLASSES):
        grw_out[c : c + 1, :] = jnp.sum(pooled * dlogits[c], axis=0, keepdims=True)
    grb_out[...] = jnp.concatenate([jnp.sum(one, axis=0) for one in dlogits])
    log_total = jnp.log(total)
    log_probs = [one - log_total for one in shifted]
    row_entropy = -sum((jnp.exp(one) * one for one in log_probs[1:]), jnp.exp(log_probs[0]) * log_probs[0])
    entropy_out[...] = jnp.sum(lengths * row_entropy, axis=0, keepdims=True) / jnp.sum(lengths, axis=0, keepdims=True)
    for copy in copies:
        copy.wait()


VMEM_LIMIT = 56 * 1024 * 1024
SECOND_LIMIT = 42 * 1024 * 1024


def local(
    hidden_in, lengths, labels,
    qkv_weight, qkv_bias, out_weight, out_bias, attention_gain, attention_shift,
    up_weight, up_bias, down_weight, down_bias, output_gain, output_shift,
    pooler_weight, pooler_bias, ramp_weight, ramp_bias,
):
    slots = lengths.shape[0]
    length = hidden_in.shape[0] // slots
    half = length // 2
    rows = slots // TILES * half
    shape = (slots, length, D)
    devices = lax.axis_size(AXES)
    sequences = hidden_in.reshape(shape)
    vectors = (qkv_bias, out_bias, attention_gain, attention_shift, up_bias, down_bias, output_gain, output_shift)
    anywhere = pl.BlockSpec(memory_space=pltpu.HBM)
    in_hbm = lambda array: pltpu.with_memory_space_constraint(array, pltpu.HBM)
    scalars = pl.BlockSpec(memory_space=pltpu.SMEM)
    vmem = pl.BlockSpec(memory_space=pltpu.VMEM)
    dma = pltpu.SemaphoreType.DMA
    weights = [pltpu.VMEM(one, bf16) for one in ((D, FF), (FF, D))]
    common = [
        pltpu.VMEM((rows * FF // D, D), bf16),
        pltpu.VMEM((slots, half, D), bf16),
    ]
    cost = pl.CostEstimate(
        flops=2 * slots * half * D * (2 * D + 2 * FF + 2 * length), bytes_accessed=30_000_000, transcendentals=0
    )
    params = pltpu.CompilerParams(vmem_limit_bytes=VMEM_LIMIT)
    hidden, later, leads, *kept = pl.pallas_call(
        first_kernel,
        name="first_half",
        out_shape=[
            pltpu.HBM(shape, bf16),
            pltpu.HBM((slots, half, D), bf16),
            pltpu.HBM((devices, slots, D + EXTRA), f32),
            pltpu.VMEM((D, D), bf16),
            pltpu.VMEM((len(vectors), FF), f32),
        ],
        in_specs=[scalars] * 2 + [anywhere] * 13,
        out_specs=[anywhere] * 3 + [vmem] * 2,
        scratch_shapes=[pltpu.VMEM(shape, bf16), pltpu.VMEM((slots, half, D), bf16)]
        + weights
        + [
            pltpu.VMEM((D, 3 * D), bf16),
            pltpu.VMEM((slots, D + EXTRA), f32),
            pltpu.VMEM((slots // TILES, half, D), bf16),
            pltpu.SMEM((slots // TILES * length // KEY_BLOCK + GROUP,), jnp.int32),
            pltpu.VMEM((2 * rows, D), bf16),
            pltpu.VMEM((2 * rows, D), bf16),
            pltpu.VMEM((2 * rows, D), bf16),
            pltpu.VMEM((slots // TILES, 8, LANES), f32),
        ]
        + [pltpu.VMEM((slots // TILES, half, D), f32)]
        + common
        + [dma((5,)), dma((slots,)), dma((slots,)), dma((len(vectors),)), dma((slots,)), dma((devices,))],
        compiler_params=params,
        cost_estimate=cost,
    )(lengths, labels, *[in_hbm(a) for a in (sequences, qkv_weight, out_weight, up_weight, down_weight, *vectors)])
    gathered = lax.all_to_all(leads, AXES, 0, 0).reshape(devices * slots, D + EXTRA)
    hidden = pl.pallas_call(
        second_kernel,
        name="second_half",
        out_shape=pltpu.HBM(shape, bf16),
        in_specs=[anywhere] * 4 + [vmem] * 2 + [anywhere],
        out_specs=anywhere,
        scratch_shapes=[pltpu.VMEM((slots, half, D), bf16)] * 2
        + weights
        + [pltpu.VMEM((slots, half, D), f32)]
        + common
        + [dma((2,)), dma((slots // 2,)), dma((slots // 2,)), dma((slots,))],
        input_output_aliases={6: 0},
        compiler_params=pltpu.CompilerParams(vmem_limit_bytes=SECOND_LIMIT),
        cost_estimate=cost,
    )(
        *[in_hbm(a) for a in (sequences, later, up_weight, down_weight)],
        *[pltpu.with_memory_space_constraint(a, pltpu.VMEM) for a in kept],
        in_hbm(hidden),
    )
    one = lambda *shape: jax.ShapeDtypeStruct(shape, f32)
    logits, gpw, gpb, grw, grb, entropy = pl.pallas_call(
        ramp_kernel,
        name="off_ramp",
        out_shape=[one(CLASSES, slots), pltpu.HBM((D, D), f32), one(D), one(CLASSES, D), one(CLASSES), one(1, 1)],
        in_specs=[vmem] * 5,
        out_specs=[vmem, anywhere] + [vmem] * 4,
        scratch_shapes=[pltpu.VMEM((devices * slots, CLASSES), f32), pltpu.VMEM((D, D), f32), dma((D // QUAD,))],
        compiler_params=pltpu.CompilerParams(vmem_limit_bytes=8 * 1024 * 1024 + 5 * 4 * gathered.size),
    )(gathered, pooler_weight, pooler_bias, ramp_weight.T, ramp_bias)
    return hidden.reshape(hidden_in.shape), logits.T, gpw, gpb, grw.T, grb, entropy.reshape(())


def solution(mesh):
    spread = P(AXES)
    placed = (P(AXES, None), spread, spread) + (P(),) * 16
    return jax.shard_map(
        local,
        mesh=mesh,
        in_specs=placed,
        out_specs=(P(AXES, None), P(AXES, None), P(), P(), P(), P(), P()),
        check_vma=False,
    )
```
